512 devices in a mesh: row: 16 (over z_lo, x, core), col: 8 (over y), depth: 4 (over z_hi).
Axes of the slice: x: 4, y: 8, z: 8 (z_hi: 4, z_lo: 2; z = z_hi * 2 + z_lo), core: 2. Of those that a mesh axis runs over, the one named last changes fastest.
Arguments:
- density: bfloat16 [2048, 64, 4096], P(('row', 'col'), None, 'depth'), as said below
- pattern: int32 [2048, 64], P(('row', 'col'), 'depth'), may hold values from 0 to 1, as said below
- keep_filter: int32 [2048, 16], P(('row', 'col'), 'depth'), may hold values from 0 to 1, as said below
Outputs:
- square: bfloat16 [2048, 64, 1024], P(('row', 'col'), None, 'depth')
The draws below stay inside these ranges and needn't reach their ends.
Inputs may be any that keep to these rules, and one draw needn't show every extreme that they name: density is exactly symmetric: for t of 1 or more, block (i, t) is the transpose of block ((i + t - 32) mod 2048, 64 - t). pattern is symmetric in the same sense; slot 0 is 0, and slots within 7 of slot 32 are 1. `keep_filter`: offsets below 4 are 1.
All inputs are finite; a program needn't handle non-finite values.
Results may differ from the reference program's by a relative error of at most 0.013.
Values may be sent and summed in bfloat16 or wider, within the bound.
No kernel may reach another device: no remote copies, remote signals or barrier semaphores. Data moves between devices by JAX's collectives and lax.ppermute only.
A program may use at most 64 MiB of HBM per device.

```python
import math
import jax
import jax.numpy as jnp
from jax import lax

BS = 64
HALF = 32
KEEP = 16
SLOTS = 64
NB = 2048
N_DEPTH = 4


def draw_density(key, part):
    key = jax.random.fold_in(key, 3)
    spread = 0.7071 * (SLOTS * BS) ** (-0.25)

    def slot_values(slot_key):
        return jax.random.normal(slot_key, (NB, BS, BS), jnp.float32)

    def one_slot(slot):
        mirror_slot = (SLOTS - slot) % SLOTS
        mine = slot_values(jax.random.fold_in(key, slot))
        theirs = slot_values(jax.random.fold_in(key, mirror_slot))
        theirs = jnp.roll(theirs, HALF - slot, axis=0)
        return ((mine + jnp.swapaxes(theirs, 1, 2)) * spread).astype(jnp.bfloat16)
    stacked = lax.map(one_slot, jnp.arange(SLOTS, dtype=jnp.int32))
    return jnp.transpose(stacked, (1, 2, 0, 3)).reshape(NB, BS, SLOTS * BS)


def draw_pattern(key, part):
    key = jax.random.fold_in(key, 1)
    coins = jax.random.randint(key, (NB, HALF), 0, 100, dtype=jnp.int32)
    offsets = jnp.arange(HALF, dtype=jnp.int32)
    upper = jnp.where((offsets[None, :] < HALF // 4) | (coins < 85), 1, 0).astype(jnp.int32)
    row_ids = jnp.arange(NB, dtype=jnp.int32)
    lower_rows = ((row_ids[:, None] - offsets[None, :]) % NB).astype(jnp.int32)
    lower = upper[lower_rows, jnp.broadcast_to(offsets[None, :], (NB, HALF))]
    lower_slots = lower[:, 1:][:, ::-1]
    first_slot = jnp.zeros((NB, 1), jnp.int32)
    return jnp.concatenate([first_slot, lower_slots, upper], axis=1)


def draw_keep_filter(key, part):
    key = jax.random.fold_in(key, 2)
    coins = jax.random.randint(key, (NB, KEEP), 0, 100, dtype=jnp.int32)
    offsets = jnp.arange(KEEP, dtype=jnp.int32)
    return jnp.where((offsets[None, :] < KEEP // 4) | (coins < 80), 1, 0).astype(jnp.int32)


def setup_inputs(seed: int = 0) -> dict:
    splits = jax.random.split(jax.random.key(seed), 4)
    density = draw_density(jax.random.fold_in(splits[3], 71), 0)
    pattern = draw_pattern(jax.random.fold_in(splits[3], 71), 0)
    keep_filter = draw_keep_filter(jax.random.fold_in(splits[3], 71), 0)
    return dict(density=density, pattern=pattern, keep_filter=keep_filter)


def spread_blocks(block_mask, block_side):
    row_count, slot_count = block_mask.shape
    spread = jnp.broadcast_to(block_mask[:, None, :, None], (row_count, block_side, slot_count, block_side))
    return spread.reshape(row_count, block_side, slot_count * block_side)


def reference(density, pattern, keep_filter):
    masked = density * spread_blocks(pattern.astype(jnp.bfloat16), BS)
    step_rows = math.gcd(NB, 64)
    share_cols = (SLOTS // N_DEPTH) * BS

    def rows_block(start):
        picked = ((start + jnp.arange(step_rows + KEEP - 1, dtype=jnp.int32)) % NB).astype(jnp.int32)
        band_slab = jnp.take(masked, picked, axis=0).astype(jnp.float32)
        own_rows = band_slab[:step_rows].reshape(step_rows, BS, N_DEPTH, share_cols)
        pieces = []
        for offset in range(KEEP):
            partner = band_slab[offset:offset + step_rows, :, :(SLOTS - offset) * BS]
            partner = jnp.pad(partner, ((0, 0), (0, 0), (offset * BS, 0)))
            partner = partner.reshape(step_rows, BS, N_DEPTH, share_cols)
            shares = jnp.einsum("iaqb,icqb->iqac", own_rows, partner, precision=lax.Precision.HIGHEST)
            shares = shares.astype(jnp.bfloat16).astype(jnp.float32)
            pieces.append(jnp.sum(shares, axis=1))
        return jnp.concatenate(pieces, axis=2)

    starts = jnp.arange(0, NB, step_rows, dtype=jnp.int32)
    product = lax.map(rows_block, starts).reshape(NB, BS, KEEP * BS)
    keep_mask = spread_blocks(keep_filter.astype(jnp.float32), BS)
    return (product * keep_mask).astype(jnp.bfloat16)
```

```python
import functools
import jax
import jax.numpy as jnp
from jax import lax
from jax.experimental import pallas as pl
from jax.experimental.pallas import tpu as pltpu
from jax.sharding import PartitionSpec as P

BS = 64
ROWS = 16
WIDE = ROWS * BS
TILE = 256
AXES = ("row", "col", "depth")
NT = (((1,), (1,)), ((), ()))
NN = (((1,), (0,)), ((), ()))


def dot(a, b, dims):
    return lax.dot_general(a, b, dims, preferred_element_type=jnp.float32)


def expand(flags, cols):
    count = flags.shape[1]
    slot = lax.broadcasted_iota(jnp.int32, (count, cols), 0)
    col = lax.broadcasted_iota(jnp.int32, (count, cols), 1)
    spread = jnp.where((col >= slot * BS) & (col < slot * BS + BS), 1.0, 0.0)
    return dot(flags.astype(jnp.float32), spread, NN)


def masked_lanes(dens, mask, i, lo, hi):
    m = jnp.broadcast_to(mask[i : i + 1, lo:hi], (16, hi - lo)).astype(jnp.bfloat16)
    x = dens[i, :, lo:hi].reshape(BS // 16, 16, hi - lo)
    return (x * m[None]).reshape(BS, hi - lo)


def upper_width(i):
    return WIDE - 128 * (i // 2)


def upper_place(i):
    a, e = i // 2, i % 2
    if a < 4:
        return i, 0
    if a == 4:
        return 8, 512 * e
    return 2 * (8 - a) + e, 128 * a


def lower_width(i):
    return 128 * ((i - 1) // 2 + 1)


def lower_place(i):
    a, e = (i - 1) // 2, (i - 1) % 2
    if i == ROWS - 1:
        return 7, 0
    if a < 3:
        return 2 * a + e, WIDE - 128 * (a + 1)
    if a == 3:
        return 6, 512 * e
    return 2 * (6 - a) + e, 0


def pack_kernel(dens, pat, send_a, send_b, mask):
    q = lax.axis_index("depth")
    mask[...] = expand(pat[...], WIDE)

    for i in range(ROWS):
        width = upper_width(i)
        row, lane = upper_place(i)
        part = masked_lanes(dens, mask, i, 0, width)
        send_b[row, :, lane : lane + width] = part

        @pl.when(q != 2)
        def _():
            send_a[row, :, lane : lane + width] = part

    @pl.when(q == 2)
    def _():
        for i in range(1, ROWS):
            width = lower_width(i)
            row, lane = lower_place(i)
            send_a[row, :, lane : lane + width] = masked_lanes(dens, mask, i, WIDE - width, WIDE)
        send_a[8] = jnp.zeros((BS, WIDE), jnp.bfloat16)


def main_kernel(dens, pat, buf_a, buf_b, own, out1, out2, out3, mask, z, y):
    q = lax.axis_index("depth")
    mask[...] = expand(pat[...], WIDE)
    outs = (own, out1, out2, out3)

    def own_upper(i):
        return masked_lanes(dens, mask, i, 0, upper_width(i))

    def own_lower(i):
        return masked_lanes(dens, mask, i, WIDE - lower_width(i), WIDE)

    def sent_upper(buf):
        def get(i):
            row, lane = upper_place(i)
            return buf[row, :, lane : lane + upper_width(i)]

        return get

    def sent_lower(buf):
        def get(i):
            row, lane = lower_place(i)
            return buf[row, :, lane : lane + lower_width(i)]

        return get

    def build(dst, base, lower, upper):
        for i in range(ROWS):
            parts = []
            if i > 0:
                width = lower_width(i)
                parts.append(lower(i) if lower else jnp.zeros((BS, width), jnp.bfloat16))
            width = upper_width(i)
            parts.append(upper(i) if upper else jnp.zeros((BS, width), jnp.bfloat16))
            both = jnp.concatenate(parts, axis=1) if i > 0 else parts[0]
            if i % 2:
                both = both[:, BS : BS + WIDE]
            if not lower and i % 2:
                lane = lax.broadcasted_iota(jnp.int32, (BS, WIDE), 1)
                both = jnp.where(lane >= i * BS, both, jnp.zeros_like(both))
            if not upper and i % 2:
                lane = lax.broadcasted_iota(jnp.int32, (BS, WIDE), 1)
                both = jnp.where(lane < i * BS, both, jnp.zeros_like(both))
            dst[base + i * BS : base + (i + 1) * BS, :] = both

    def mirror(dst, base):
        r = lax.broadcasted_iota(jnp.int32, (TILE, TILE), 0)
        c = lax.broadcasted_iota(jnp.int32, (TILE, TILE), 1)
        eye = jnp.where(r == c, 1.0, 0.0).astype(jnp.bfloat16)
        strict = jnp.where(r // BS < c // BS, 1.0, 0.0).astype(jnp.bfloat16)
        for n in range(WIDE // TILE):
            rows = slice(base + n * TILE, base + (n + 1) * TILE)
            cols = slice(n * TILE, (n + 1) * TILE)
            diag = dst[rows, cols]
            dst[rows, cols] = diag + dot(eye, diag * strict, NT).astype(jnp.bfloat16)
            for m in range(n + 1, WIDE // TILE):
                tile = dst[rows, m * TILE : (m + 1) * TILE]
                dst[base + m * TILE : base + (m + 1) * TILE, cols] = dot(eye, tile, NT).astype(jnp.bfloat16)

    def finish(static_q, tile_row, window):
        for n in range(TILE // BS):
            i = tile_row * (TILE // BS) + n
            row = window[n * BS : (n + 1) * BS, n * BS : n * BS + WIDE].astype(jnp.bfloat16)
            for p in range(4):
                outs[(p - static_q) % 4][i] = row[:, p * TILE : (p + 1) * TILE]

    def products(static_q):
        for t in range(WIDE // TILE):
            lo, hi = t * TILE, (t + 1) * TILE
            depth_hi = hi if static_q == 3 else WIDE
            window = dot(z[lo:hi, :depth_hi], z[lo : lo + WIDE + TILE, :depth_hi], NT)
            if static_q == 0:
                first = dot(y[lo:hi, lo:], y[lo:, lo:], NT)
                window = jnp.concatenate(
                    [window[:, : WIDE - lo] + first, window[:, WIDE - lo :]], axis=1
                )
            if static_q == 2:
                first = dot(y[lo:hi, :], y[lo:, :], NT)
                second = dot(y[lo:hi, :], z[:WIDE, :hi], NN)
                window = window + jnp.concatenate([first, second], axis=1)
            finish(static_q, t, window)

    @pl.when(q == 0)
    def _():
        build(z, 0, own_lower, sent_upper(buf_a))
        build(z, WIDE, None, sent_upper(buf_b))
        build(y, 0, None, own_upper)
        products(0)

    @pl.when(q == 1)
    def _():
        own[...] = jnp.zeros_like(own)

    @pl.when(q == 2)
    def _():
        build(z, 0, own_lower, sent_upper(buf_a))
        build(z, WIDE, None, sent_upper(buf_b))
        mirror(z, WIDE)
        build(y, 0, None, own_upper)
        mirror(y, 0)
        products(2)

    @pl.when(q == 3)
    def _():
        build(z, 0, own_lower, None)
        build(z, WIDE, sent_lower(buf_a), sent_upper(buf_b))
        products(3)


def final_kernel(own, in1, in2, in3, keep, out, mask):
    mask[...] = expand(keep[...], TILE)
    for i in range(ROWS):
        total = own[i].astype(jnp.float32) + in1[i].astype(jnp.float32)
        total = total + in2[i].astype(jnp.float32) + in3[i].astype(jnp.float32)
        out[i] = (total * mask[i : i + 1, :]).astype(jnp.bfloat16)


def vmem(count):
    return [pl.BlockSpec(memory_space=pltpu.VMEM)] * count


def per_device(groups, density, pattern, keep_filter):
    packed = jax.ShapeDtypeStruct((9, BS, WIDE), jnp.bfloat16)
    share = jax.ShapeDtypeStruct((ROWS, BS, TILE), jnp.bfloat16)
    mib = 1024 * 1024

    send_a, send_b = pl.pallas_call(
        pack_kernel,
        out_shape=(packed, packed),
        in_specs=vmem(2),
        out_specs=tuple(vmem(2)),
        scratch_shapes=[pltpu.VMEM((ROWS, WIDE), jnp.float32)],
        compiler_params=pltpu.CompilerParams(vmem_limit_bytes=24 * mib),
        cost_estimate=pl.CostEstimate(flops=4_000_000, bytes_accessed=4_500_000, transcendentals=0),
    )(density, pattern)

    def device(g, q):
        return (g % groups) * 4 + q

    route_a, route_b = [], []
    for g in range(groups):
        route_a += [(device(g, 1), device(g, 0)), (device(g, 3), device(g, 2))]
        route_a += [(device(g + 1, 2), device(g, 3))]
        route_b += [(device(g + 1, q), device(g, q)) for q in (0, 2, 3)]
    buf_a = lax.ppermute(send_a, AXES, route_a)
    buf_b = lax.ppermute(send_b, AXES, route_b)

    parts = pl.pallas_call(
        main_kernel,
        out_shape=(share,) * 4,
        in_specs=vmem(4),
        out_specs=tuple(vmem(4)),
        scratch_shapes=[
            pltpu.VMEM((ROWS, WIDE), jnp.float32),
            pltpu.VMEM((2 * WIDE, WIDE), jnp.bfloat16),
            pltpu.VMEM((WIDE, WIDE), jnp.bfloat16),
        ],
        compiler_params=pltpu.CompilerParams(vmem_limit_bytes=40 * mib),
        cost_estimate=pl.CostEstimate(flops=8_000_000_000, bytes_accessed=7_000_000, transcendentals=0),
    )(density, pattern, buf_a, buf_b)

    landed = [parts[0]]
    for shift in (1, 2, 3):
        route = [(q, (q + shift) % 4) for q in (0, 2, 3)]
        landed.append(lax.ppermute(parts[shift], "depth", route))

    return pl.pallas_call(
        final_kernel,
        out_shape=share,
        in_specs=vmem(5),
        out_specs=pl.BlockSpec(memory_space=pltpu.VMEM),
        scratch_shapes=[pltpu.VMEM((ROWS, TILE), jnp.float32)],
        compiler_params=pltpu.CompilerParams(vmem_limit_bytes=16 * mib),
        cost_estimate=pl.CostEstimate(flops=1_500_000, bytes_accessed=2_700_000, transcendentals=0),
    )(*landed, keep_filter)


def solution(mesh):
    placed = (
        P(("row", "col"), None, "depth"),
        P(("row", "col"), "depth"),
        P(("row", "col"), "depth"),
    )
    groups = mesh.shape["row"] * mesh.shape["col"]
    return jax.shard_map(
        functools.partial(per_device, groups),
        mesh=mesh,
        in_specs=placed,
        out_specs=P(("row", "col"), None, "depth"),
        check_vma=False,
    )
```

```python
import functools
import jax
import jax.numpy as jnp
from jax import lax
from jax.experimental import pallas as pl
from jax.experimental.pallas import tpu as pltpu
from jax.sharding import PartitionSpec as P

BS = 64
ROWS = 16
WIDE = ROWS * BS
HALF = WIDE // 2
TILE = 256
AXES = ("row", "col", "depth")
NT = (((1,), (1,)), ((), ()))
NN = (((1,), (0,)), ((), ()))


def dot(a, b, dims):
    return lax.dot_general(a, b, dims, preferred_element_type=jnp.float32)


def expand(flags, cols):
    count = flags.shape[1]
    slot = lax.broadcasted_iota(jnp.int32, (count, cols), 0)
    col = lax.broadcasted_iota(jnp.int32, (count, cols), 1)
    spread = jnp.where((col >= slot * BS) & (col < slot * BS + BS), 1.0, 0.0)
    return dot(flags.astype(jnp.float32), spread, NN)


def masked_lanes(dens, mask, i, lo, hi):
    m = jnp.broadcast_to(mask[i : i + 1, lo:hi], (16, hi - lo)).astype(jnp.bfloat16)
    x = dens[i, :, lo:hi].reshape(BS // 16, 16, hi - lo)
    return (x * m[None]).reshape(BS, hi - lo)


def upper_width(i):
    return WIDE - 128 * (i // 2)


def lower_width(i):
    return 128 * ((i - 1) // 2 + 1)


def lower_place(i):
    a, e = (i - 1) // 2, (i - 1) % 2
    width = lower_width(i)
    if a < 3:
        return [(2 * (2 * a + e) + 1, HALF - width, 0, width)]
    if a == 3:
        return [(12 + e, 0, 0, width)]
    row = 7 if i == ROWS - 1 else 2 * (6 - a) + e
    return [(2 * row, 0, 0, HALF), (2 * row + 1, 0, HALF, width - HALF)]


def pack_kernel(dens, pat, send_a, send_b, mask):
    q = lax.axis_index("depth")
    mask[...] = expand(pat[...], WIDE)

    def put(n, lo, hi, part):
        send_b[n, :, lo:hi] = part

        @pl.when(q != 2)
        def _():
            send_a[n, :, lo:hi] = part

    def own(i, lo, hi):
        return masked_lanes(dens, mask, i, lo, hi)

    put(0, 0, HALF, own(0, 0, HALF))
    put(1, 0, HALF, own(0, HALF, WIDE))
    for i in range(1, 8):
        put(1 + i, 0, HALF, own(i, 0, HALF))
        split = HALF - BS * i
        left = own(i, HALF, WIDE - 128 * (i // 2))[:, :split]
        right = own(ROWS - i, 0, 128 * ((i + 1) // 2))[:, : BS * i]
        put(9 + i, 0, HALF, jnp.concatenate([left, right], axis=1))
    put(9, 0, HALF, own(8, 0, HALF))

    @pl.when(q == 2)
    def _():
        for i in range(1, ROWS):
            width = lower_width(i)
            part = own(i, WIDE - width, WIDE)
            for n, lane, first, lanes in lower_place(i):
                send_a[n, :, lane : lane + lanes] = part[:, first : first + lanes]
        send_a[16] = jnp.zeros((BS, HALF), jnp.bfloat16)


def own_parts(dens, mask):
    def upper(i):
        return masked_lanes(dens, mask, i, 0, upper_width(i))

    def lower(i):
        return masked_lanes(dens, mask, i, WIDE - lower_width(i), WIDE)

    return lower, upper


def sent_upper(buf):
    def get(i):
        if i == 0:
            return jnp.concatenate([buf[0], buf[1]], axis=1)
        if i < 8:
            rest = HALF - 128 * (i // 2)
            if rest == 0:
                return buf[1 + i]
            return jnp.concatenate([buf[1 + i], buf[9 + i, :, :rest]], axis=1)
        return buf[9 + ROWS - i if i > 8 else 9]

    return get


def sent_lower(buf):
    def get(i):
        pieces = [buf[n, :, lane : lane + lanes] for n, lane, _, lanes in lower_place(i)]
        return pieces[0] if len(pieces) == 1 else jnp.concatenate(pieces, axis=1)

    return get


def build(dst, base, lower, upper, packed=False):
    lane = lax.broadcasted_iota(jnp.int32, (BS, WIDE), 1)
    for i in range(ROWS):
        rows = slice(base + i * BS, base + (i + 1) * BS)
        parts = []
        if i > 0:
            parts.append(lower(i) if lower else jnp.zeros((BS, lower_width(i)), jnp.bfloat16))
        placed = packed and i >= 8
        if upper and not placed:
            parts.append(upper(i))
        else:
            parts.append(jnp.zeros((BS, upper_width(i)), jnp.bfloat16))
        both = jnp.concatenate(parts, axis=1) if i > 0 else parts[0]
        if i % 2:
            both = both[:, BS : BS + WIDE]
            if not lower:
                both = jnp.where(lane >= i * BS, both, jnp.zeros_like(both))
            if not upper or placed:
                both = jnp.where(lane < i * BS, both, jnp.zeros_like(both))
        if placed:
            dst[rows, :HALF] = both[:, :HALF]
            right = jnp.where(lane[:, HALF:] >= i * BS, upper(i), both[:, HALF:])
            dst[rows, HALF:] = right
        else:
            dst[rows, :] = both


def mirror(dst, base):
    r = lax.broadcasted_iota(jnp.int32, (TILE, TILE), 0)
    c = lax.broadcasted_iota(jnp.int32, (TILE, TILE), 1)
    eye = jnp.where(r == c, 1.0, 0.0).astype(jnp.bfloat16)
    above = lax.shift_right_logical(r, 6) < lax.shift_right_logical(c, 6)
    strict = jnp.where(above, 1.0, 0.0).astype(jnp.bfloat16)
    for n in range(WIDE // TILE):
        rows = slice(base + n * TILE, base + (n + 1) * TILE)
        cols = slice(n * TILE, (n + 1) * TILE)
        diag = dst[rows, cols]
        dst[rows, cols] = diag + dot(eye, diag * strict, NT).astype(jnp.bfloat16)
        for m in range(n + 1, WIDE // TILE):
            tile = dst[rows, m * TILE : (m + 1) * TILE]
            turned = dot(eye, tile, NT).astype(jnp.bfloat16)
            dst[base + m * TILE : base + (m + 1) * TILE, cols] = turned


def prepare_kernel(dens, pat, y, mask):
    q = lax.axis_index("depth")

    @pl.when((q == 0) | (q == 2))
    def _():
        mask[...] = expand(pat[...], WIDE)
        build(y, 0, None, own_parts(dens, mask)[1])

    @pl.when(q == 2)
    def _():
        mirror(y, 0)


def main_kernel(dens, pat, y, buf_a, buf_b, own, up1, down1, up2, down2, mask, z):
    q = lax.axis_index("depth")
    mask[...] = expand(pat[...], WIDE)
    own_lower, own_upper = own_parts(dens, mask)

    def finish(static_q, tile_row, window):
        for n in range(TILE // BS):
            i = tile_row * (TILE // BS) + n
            row = window[n * BS : (n + 1) * BS, n * BS : n * BS + WIDE].astype(jnp.bfloat16)

            def share(p):
                p = p % 4
                return row[:, p * TILE : (p + 1) * TILE]

            own[i] = share(static_q)
            up2[i] = share(static_q + 1)
            down2[i] = share(static_q - 1)
            if i < 8:
                up1[i] = share(static_q + 2)
            else:
                down1[i - 8] = share(static_q + 2)

    def products(static_q):
        for t in range(WIDE // TILE):
            lo, hi = t * TILE, (t + 1) * TILE
            depth_hi = hi if static_q == 3 else WIDE
            window = dot(z[lo:hi, :depth_hi], z[lo : lo + WIDE + TILE, :depth_hi], NT)
            if static_q == 0:
                first = dot(y[lo:hi, lo:], y[lo:, lo:], NT)
                window = jnp.concatenate(
                    [window[:, : WIDE - lo] + first, window[:, WIDE - lo :]], axis=1
                )
            if static_q == 2:
                first = dot(y[lo:hi, :], y[lo:, :], NT)
                second = dot(y[lo:hi, :], z[:WIDE, :hi], NN)
                window = window + jnp.concatenate([first, second], axis=1)
            finish(static_q, t, window)

    @pl.when(q == 0)
    def _():
        build(z, 0, own_lower, sent_upper(buf_a), True)
        build(z, WIDE, None, sent_upper(buf_b), True)
        products(0)

    @pl.when(q == 1)
    def _():
        for ref in (own, up1, down1, up2, down2):
            ref[...] = jnp.zeros_like(ref)

    @pl.when(q == 2)
    def _():
        build(z, 0, own_lower, sent_upper(buf_a), True)
        build(z, WIDE, None, sent_upper(buf_b), True)
        mirror(z, WIDE)
        products(2)

    @pl.when(q == 3)
    def _():
        build(z, 0, own_lower, None)
        build(z, WIDE, sent_lower(buf_a), sent_upper(buf_b), True)
        products(3)


def add_kernel(up2, down2, got_up, got_down, up_out, down_out):
    for i in range(8):
        total = up2[i].astype(jnp.float32) + got_up[i].astype(jnp.float32)
        up_out[i] = total.astype(jnp.bfloat16)
        down_out[i] = down2[i]
        total = down2[8 + i].astype(jnp.float32) + got_down[i].astype(jnp.float32)
        down_out[8 + i] = total.astype(jnp.bfloat16)
        up_out[8 + i] = up2[8 + i]


def final_kernel(own, got_up, got_down, keep, out, mask):
    mask[...] = expand(keep[...], TILE)
    for i in range(ROWS):
        total = own[i].astype(jnp.float32) + got_up[i].astype(jnp.float32)
        total = total + got_down[i].astype(jnp.float32)
        out[i] = (total * mask[i : i + 1, :]).astype(jnp.bfloat16)


def vmem(count):
    return [pl.BlockSpec(memory_space=pltpu.VMEM)] * count


def per_device(groups, density, pattern, keep_filter):
    mib = 1024 * 1024

    def call(kernel, outs, scratch, limit, flops, moved, *operands):
        return pl.pallas_call(
            kernel,
            out_shape=tuple(jax.ShapeDtypeStruct(shape, jnp.bfloat16) for shape in outs),
            in_specs=vmem(len(operands)),
            out_specs=tuple(vmem(len(outs))),
            scratch_shapes=scratch,
            compiler_params=pltpu.CompilerParams(vmem_limit_bytes=limit * mib),
            cost_estimate=pl.CostEstimate(flops=flops, bytes_accessed=moved, transcendentals=0),
        )(*operands)

    packed = (17, BS, HALF)
    share = (ROWS, BS, TILE)
    half_share = (ROWS // 2, BS, TILE)
    slot_mask = pltpu.VMEM((ROWS, WIDE), jnp.float32)

    send_a, send_b = call(
        pack_kernel, (packed,) * 2, [slot_mask], 24, 4_000_000, 4_500_000, density, pattern
    )

    def device(g, q):
        return (g % groups) * 4 + q

    route_a, route_b = [], []
    for g in range(groups):
        route_a += [(device(g, 1), device(g, 0)), (device(g, 3), device(g, 2))]
        route_a += [(device(g + 1, 2), device(g, 3))]
        route_b += [(device(g + 1, q), device(g, q)) for q in (0, 2, 3)]
    buf_a = lax.ppermute(send_a, AXES, route_a)
    buf_b = lax.ppermute(send_b, AXES, route_b)

    (prepared,) = call(
        prepare_kernel, ((WIDE, WIDE),), [slot_mask], 24, 1_000_000_000, 4_500_000, density, pattern
    )
    own, up1, down1, up2, down2 = call(
        main_kernel,
        (share, half_share, half_share, share, share),
        [slot_mask, pltpu.VMEM((2 * WIDE, WIDE), jnp.bfloat16)],
        40,
        8_000_000_000,
        9_000_000,
        density,
        pattern,
        prepared,
        buf_a,
        buf_b,
    )

    upwards = [(q, (q + 1) % 4) for q in range(4)]
    downwards = [(q, (q - 1) % 4) for q in range(4)]
    got_up = lax.ppermute(up1, "depth", upwards)
    got_down = lax.ppermute(down1, "depth", downwards)
    up2, down2 = call(
        add_kernel, (share,) * 2, [], 16, 1_000_000, 3_000_000, up2, down2, got_up, got_down
    )
    got_up = lax.ppermute(up2, "depth", upwards)
    got_down = lax.ppermute(down2, "depth", downwards)
    (out,) = call(
        final_kernel,
        (share,),
        [pltpu.VMEM((ROWS, TILE), jnp.float32)],
        16,
        1_500_000,
        2_700_000,
        own,
        got_up,
        got_down,
        keep_filter,
    )
    return out


def solution(mesh):
    placed = (
        P(("row", "col"), None, "depth"),
        P(("row", "col"), "depth"),
        P(("row", "col"), "depth"),
    )
    groups = mesh.shape["row"] * mesh.shape["col"]
    return jax.shard_map(
        functools.partial(per_device, groups),
        mesh=mesh,
        in_specs=placed,
        out_specs=P(("row", "col"), None, "depth"),
        check_vma=False,
    )
```

```python
import functools
import jax
import jax.numpy as jnp
from jax import lax
from jax.experimental import pallas as pl
from jax.experimental.pallas import tpu as pltpu
from jax.sharding import PartitionSpec as P

BS = 64
ROWS = 16
WIDE = ROWS * BS
HALF = WIDE // 2
TILE = 256
AXES = ("row", "col", "depth")
NT = (((1,), (1,)), ((), ()))
NN = (((1,), (0,)), ((), ()))


def dot(a, b, dims):
    return lax.dot_general(a, b, dims, preferred_element_type=jnp.float32)


def expand(flags, cols):
    count = flags.shape[1]
    slot = lax.broadcasted_iota(jnp.int32, (count, cols), 0)
    col = lax.broadcasted_iota(jnp.int32, (count, cols), 1)
    spread = jnp.where((col >= slot * BS) & (col < slot * BS + BS), 1.0, 0.0)
    return dot(flags.astype(jnp.float32), spread, NN)


def masked_lanes(dens, mask, i, lo, hi):
    m = jnp.broadcast_to(mask[i : i + 1, lo:hi], (16, hi - lo)).astype(jnp.bfloat16)
    x = dens[i, :, lo:hi].reshape(BS // 16, 16, hi - lo)
    return (x * m[None]).reshape(BS, hi - lo)


def group_index():
    return lax.axis_index("row") * lax.axis_size("col") + lax.axis_index("col")


def late_half(groups_half):
    return group_index() >= groups_half


def upper_width(i):
    return WIDE - 128 * (i // 2)


def lower_width(i):
    return 128 * ((i - 1) // 2 + 1)


def lower_place(i):
    a, e = (i - 1) // 2, (i - 1) % 2
    width = lower_width(i)
    if a < 3:
        return [(2 * (2 * a + e) + 1, HALF - width, 0, width)]
    if a == 3:
        return [(12 + e, 0, 0, width)]
    row = 7 if i == ROWS - 1 else 2 * (6 - a) + e
    return [(2 * row, 0, 0, HALF), (2 * row + 1, 0, HALF, width - HALF)]


def pack_kernel(groups_half, dens, pat, send_1, send_2, send_3, mask):
    q = lax.axis_index("depth")
    late = late_half(groups_half)
    mask[...] = expand(pat[...], WIDE)
    upper_first = (q != 2) | jnp.logical_not(late)
    upper_second = (q != 2) | late

    def put(n, part):
        send_3[n] = part

        @pl.when(upper_first)
        def _():
            send_1[n] = part

        @pl.when(upper_second)
        def _():
            send_2[n] = part

    def own(i, lo, hi):
        return masked_lanes(dens, mask, i, lo, hi)

    put(0, own(0, 0, HALF))
    put(1, own(0, HALF, WIDE))
    for i in range(1, 8):
        put(1 + i, own(i, 0, HALF))
        split = HALF - BS * i
        left = own(i, HALF, WIDE - 128 * (i // 2))[:, :split]
        right = own(ROWS - i, 0, 128 * ((i + 1) // 2))[:, : BS * i]
        put(9 + i, jnp.concatenate([left, right], axis=1))
    put(9, own(8, 0, HALF))

    def put_lower(dst):
        for i in range(1, ROWS):
            width = lower_width(i)
            part = own(i, WIDE - width, WIDE)
            for n, lane, first, lanes in lower_place(i):
                dst[n, :, lane : lane + lanes] = part[:, first : first + lanes]
        dst[16] = jnp.zeros((BS, HALF), jnp.bfloat16)

    @pl.when(jnp.logical_not(upper_first))
    def _():
        put_lower(send_1)

    @pl.when(jnp.logical_not(upper_second))
    def _():
        put_lower(send_2)


def own_parts(dens, mask):
    def upper(i):
        return masked_lanes(dens, mask, i, 0, upper_width(i))

    def lower(i):
        return masked_lanes(dens, mask, i, WIDE - lower_width(i), WIDE)

    return lower, upper


def chosen(pick, first, second, third=None, pick_third=None):
    def get(n, lo, hi):
        part = jnp.where(pick, first[n, :, lo:hi], second[n, :, lo:hi])
        if third is not None:
            part = jnp.where(pick_third, third[n, :, lo:hi], part)
        return part

    return get


def sent_upper(buf):
    def get(i):
        if i == 0:
            return jnp.concatenate([buf(0, 0, HALF), buf(1, 0, HALF)], axis=1)
        if i < 8:
            rest = HALF - 128 * (i // 2)
            return jnp.concatenate([buf(1 + i, 0, HALF), buf(9 + i, 0, rest)], axis=1)
        return buf(9 + ROWS - i if i > 8 else 9, 0, HALF)

    return get


def sent_lower(buf):
    def get(i):
        pieces = [buf(n, lane, lane + lanes) for n, lane, _, lanes in lower_place(i)]
        return pieces[0] if len(pieces) == 1 else jnp.concatenate(pieces, axis=1)

    return get


def build(dst, base, lower, upper, packed=False):
    lane = lax.broadcasted_iota(jnp.int32, (BS, WIDE), 1)
    for i in range(ROWS):
        rows = slice(base + i * BS, base + (i + 1) * BS)
        parts = []
        if i > 0:
            parts.append(lower(i) if lower else jnp.zeros((BS, lower_width(i)), jnp.bfloat16))
        placed = packed and i >= 8
        if upper and not placed:
            parts.append(upper(i))
        else:
            parts.append(jnp.zeros((BS, upper_width(i)), jnp.bfloat16))
        both = jnp.concatenate(parts, axis=1) if i > 0 else parts[0]
        if i % 2:
            both = both[:, BS : BS + WIDE]
            if not lower:
                both = jnp.where(lane >= i * BS, both, jnp.zeros_like(both))
            if not upper or placed:
                both = jnp.where(lane < i * BS, both, jnp.zeros_like(both))
        if placed:
            dst[rows, :HALF] = both[:, :HALF]
            right = jnp.where(lane[:, HALF:] >= i * BS, upper(i), both[:, HALF:])
            dst[rows, HALF:] = right
        else:
            dst[rows, :] = both


def mirror(dst, base):
    r = lax.broadcasted_iota(jnp.int32, (TILE, TILE), 0)
    c = lax.broadcasted_iota(jnp.int32, (TILE, TILE), 1)
    eye = jnp.where(r == c, 1.0, 0.0).astype(jnp.bfloat16)
    above = lax.shift_right_logical(r, 6) < lax.shift_right_logical(c, 6)
    strict = jnp.where(above, 1.0, 0.0).astype(jnp.bfloat16)
    for n in range(WIDE // TILE):
        rows = slice(base + n * TILE, base + (n + 1) * TILE)
        cols = slice(n * TILE, (n + 1) * TILE)
        diag = dst[rows, cols]
        dst[rows, cols] = diag + dot(eye, diag * strict, NT).astype(jnp.bfloat16)
        for m in range(n + 1, WIDE // TILE):
            tile = dst[rows, m * TILE : (m + 1) * TILE]
            turned = dot(eye, tile, NT).astype(jnp.bfloat16)
            dst[base + m * TILE : base + (m + 1) * TILE, cols] = turned


def prepare_kernel(dens, pat, y, mask):
    q = lax.axis_index("depth")

    @pl.when((q == 0) | (q == 2))
    def _():
        mask[...] = expand(pat[...], WIDE)
        build(y, 0, None, own_parts(dens, mask)[1])

    @pl.when(q == 2)
    def _():
        mirror(y, 0)


def main_kernel(groups, dens, pat, y, got_1, got_2, got_3, own, up1, down1, up2, down2, mask, z):
    q = lax.axis_index("depth")
    late = late_half(groups // 2)
    group = group_index()
    turn = (group == groups - 1) | (group == groups // 2 - 1)
    next_late = late != turn
    mask[...] = expand(pat[...], WIDE)
    own_lower, own_upper = own_parts(dens, mask)

    def finish(static_q, tile_row, window):
        for n in range(TILE // BS):
            i = tile_row * (TILE // BS) + n
            row = window[n * BS : (n + 1) * BS, n * BS : n * BS + WIDE].astype(jnp.bfloat16)

            def share(p):
                p = p % 4
                return row[:, p * TILE : (p + 1) * TILE]

            own[i] = share(static_q)
            up2[i] = share(static_q + 1)
            down2[i] = share(static_q - 1)
            if i < 8:
                up1[i] = share(static_q + 2)
            else:
                down1[i - 8] = share(static_q + 2)

    def products(static_q):
        for t in range(WIDE // TILE):
            lo, hi = t * TILE, (t + 1) * TILE
            depth_hi = hi if static_q == 3 else WIDE
            window = dot(z[lo:hi, :depth_hi], z[lo : lo + WIDE + TILE, :depth_hi], NT)
            if static_q == 0:
                first = dot(y[lo:hi, lo:], y[lo:, lo:], NT)
                window = jnp.concatenate(
                    [window[:, : WIDE - lo] + first, window[:, WIDE - lo :]], axis=1
                )
            if static_q == 2:
                first = dot(y[lo:hi, :], y[lo:, :], NT)
                second = dot(y[lo:hi, :], z[:WIDE, :hi], NN)
                window = window + jnp.concatenate([first, second], axis=1)
            finish(static_q, t, window)

    @pl.when(q == 0)
    def _():
        build(z, 0, own_lower, sent_upper(chosen(late, got_1, got_2)), True)
        build(z, WIDE, None, sent_upper(chosen(late, got_2, got_1)), True)
        products(0)

    @pl.when(q == 1)
    def _():
        for ref in (own, up1, down1, up2, down2):
            ref[...] = jnp.zeros_like(ref)

    @pl.when(q == 2)
    def _():
        build(z, 0, own_lower, sent_upper(chosen(late, got_1, got_2)), True)
        build(z, WIDE, None, sent_upper(chosen(late, got_2, got_1, got_3, turn)), True)
        mirror(z, WIDE)
        products(2)

    @pl.when(q == 3)
    def _():
        build(z, 0, own_lower, None)
        lower = sent_lower(chosen(next_late, got_1, got_2))
        build(z, WIDE, lower, sent_upper(chosen(next_late, got_2, got_1)), True)
        products(3)


def add_kernel(up2, down2, got_up, got_down, up_out, down_out):
    for i in range(8):
        total = up2[i].astype(jnp.float32) + got_up[i].astype(jnp.float32)
        up_out[i] = total.astype(jnp.bfloat16)
        down_out[i] = down2[i]
        total = down2[8 + i].astype(jnp.float32) + got_down[i].astype(jnp.float32)
        down_out[8 + i] = total.astype(jnp.bfloat16)
        up_out[8 + i] = up2[8 + i]


def final_kernel(own, got_up, got_down, keep, out, mask):
    mask[...] = expand(keep[...], TILE)
    for i in range(ROWS):
        total = own[i].astype(jnp.float32) + got_up[i].astype(jnp.float32)
        total = total + got_down[i].astype(jnp.float32)
        out[i] = (total * mask[i : i + 1, :]).astype(jnp.bfloat16)


def vmem(count):
    return [pl.BlockSpec(memory_space=pltpu.VMEM)] * count


def per_device(groups, density, pattern, keep_filter):
    mib = 1024 * 1024

    def call(kernel, outs, scratch, limit, flops, moved, *operands):
        return pl.pallas_call(
            kernel,
            out_shape=tuple(jax.ShapeDtypeStruct(shape, jnp.bfloat16) for shape in outs),
            in_specs=vmem(len(operands)),
            out_specs=tuple(vmem(len(outs))),
            scratch_shapes=scratch,
            compiler_params=pltpu.CompilerParams(vmem_limit_bytes=limit * mib),
            cost_estimate=pl.CostEstimate(flops=flops, bytes_accessed=moved, transcendentals=0),
        )(*operands)

    packed = (17, BS, HALF)
    share = (ROWS, BS, TILE)
    half_share = (ROWS // 2, BS, TILE)
    slot_mask = pltpu.VMEM((ROWS, WIDE), jnp.float32)

    half = groups // 2
    sends = call(
        functools.partial(pack_kernel, half),
        (packed,) * 3,
        [slot_mask],
        24,
        4_000_000,
        5_500_000,
        density,
        pattern,
    )

    def device(g, q):
        return (g % groups) * 4 + q

    routes = ([], [], [])
    for g in range(groups):
        late = int(g >= half)
        over_depth, over_y = routes[1 - late], routes[late]
        over_depth += [(device(g, 1), device(g, 0)), (device(g, 3), device(g, 2))]
        over_depth += [(device(g, 2), device(g - 1, 3))]
        over_y += [(device(g, 3), device(g - 1, 3))]
        turn = g in (0, half)
        routes[1 - late if turn else late].append((device(g, 0), device(g - 1, 0)))
        routes[2 if turn else late].append((device(g, 2), device(g - 1, 2)))
    got = [lax.ppermute(sent, AXES, route) for sent, route in zip(sends, routes)]

    (prepared,) = call(
        prepare_kernel, ((WIDE, WIDE),), [slot_mask], 24, 1_000_000_000, 4_500_000, density, pattern
    )
    own, up1, down1, up2, down2 = call(
        functools.partial(main_kernel, groups),
        (share, half_share, half_share, share, share),
        [slot_mask, pltpu.VMEM((2 * WIDE, WIDE), jnp.bfloat16)],
        40,
        8_000_000_000,
        10_000_000,
        density,
        pattern,
        prepared,
        *got,
    )

    upwards = [(q, (q + 1) % 4) for q in range(4)]
    downwards = [(q, (q - 1) % 4) for q in range(4)]
    got_up = lax.ppermute(up1, "depth", upwards)
    got_down = lax.ppermute(down1, "depth", downwards)
    up2, down2 = call(
        add_kernel, (share,) * 2, [], 16, 1_000_000, 3_000_000, up2, down2, got_up, got_down
    )
    got_up = lax.ppermute(up2, "depth", upwards)
    got_down = lax.ppermute(down2, "depth", downwards)
    (out,) = call(
        final_kernel,
        (share,),
        [pltpu.VMEM((ROWS, TILE), jnp.float32)],
        16,
        1_500_000,
        2_700_000,
        own,
        got_up,
        got_down,
        keep_filter,
    )
    return out


def solution(mesh):
    placed = (
        P(("row", "col"), None, "depth"),
        P(("row", "col"), "depth"),
        P(("row", "col"), "depth"),
    )
    groups = mesh.shape["row"] * mesh.shape["col"]
    return jax.shard_map(
        functools.partial(per_device, groups),
        mesh=mesh,
        in_specs=placed,
        out_specs=P(("row", "col"), None, "depth"),
        check_vma=False,
    )
```

```python
import functools
import jax
import jax.numpy as jnp
from jax import lax
from jax.experimental import pallas as pl
from jax.experimental.pallas import tpu as pltpu
from jax.sharding import PartitionSpec as P

BS = 64
ROWS = 16
WIDE = ROWS * BS
HALF = WIDE // 2
TILE = 256
AXES = ("row", "col", "depth")
NT = (((1,), (1,)), ((), ()))
NN = (((1,), (0,)), ((), ()))


def dot(a, b, dims):
    return lax.dot_general(a, b, dims, preferred_element_type=jnp.float32)


def expand(flags, cols):
    count = flags.shape[1]
    slot = lax.broadcasted_iota(jnp.int32, (count, cols), 0)
    col = lax.broadcasted_iota(jnp.int32, (count, cols), 1)
    spread = jnp.where((col >= slot * BS) & (col < slot * BS + BS), 1.0, 0.0)
    return dot(flags.astype(jnp.float32), spread, NN)


def masked_lanes(dens, mask, i, lo, hi):
    m = jnp.broadcast_to(mask[i : i + 1, lo:hi], (16, hi - lo)).astype(jnp.bfloat16)
    x = dens[i, :, lo:hi].reshape(BS // 16, 16, hi - lo)
    return (x * m[None]).reshape(BS, hi - lo)


def group_index():
    return lax.axis_index("row") * lax.axis_size("col") + lax.axis_index("col")


def late_half(groups_half):
    return group_index() >= groups_half


def upper_width(i):
    return WIDE - 128 * (i // 2)


def lower_width(i):
    return 128 * ((i - 1) // 2 + 1)


def lower_place(i):
    a, e = (i - 1) // 2, (i - 1) % 2
    width = lower_width(i)
    if a < 3:
        return [(2 * (2 * a + e) + 1, HALF - width, 0, width)]
    if a == 3:
        return [(12 + e, 0, 0, width)]
    row = 7 if i == ROWS - 1 else 2 * (6 - a) + e
    return [(2 * row, 0, 0, HALF), (2 * row + 1, 0, HALF, width - HALF)]


def pack_kernel(groups_half, dens, pat, send_1, send_2, mask):
    q = lax.axis_index("depth")
    late = late_half(groups_half)
    mask[...] = expand(pat[...], WIDE)
    upper_first = (q != 2) | late
    upper_second = (q != 2) | jnp.logical_not(late)

    def put(n, part):
        @pl.when(upper_first)
        def _():
            send_1[n] = part

        @pl.when(upper_second)
        def _():
            send_2[n] = part

    def own(i, lo, hi):
        return masked_lanes(dens, mask, i, lo, hi)

    put(0, own(0, 0, HALF))
    put(1, own(0, HALF, WIDE))
    for i in range(1, 8):
        put(1 + i, own(i, 0, HALF))
        split = HALF - BS * i
        left = own(i, HALF, WIDE - 128 * (i // 2))[:, :split]
        right = own(ROWS - i, 0, 128 * ((i + 1) // 2))[:, : BS * i]
        put(9 + i, jnp.concatenate([left, right], axis=1))
    put(9, own(8, 0, HALF))

    def put_lower(dst):
        for i in range(1, ROWS):
            width = lower_width(i)
            part = own(i, WIDE - width, WIDE)
            for n, lane, first, lanes in lower_place(i):
                dst[n, :, lane : lane + lanes] = part[:, first : first + lanes]
        dst[16] = jnp.zeros((BS, HALF), jnp.bfloat16)

    @pl.when(jnp.logical_not(upper_first))
    def _():
        put_lower(send_1)

    @pl.when(jnp.logical_not(upper_second))
    def _():
        put_lower(send_2)


def own_parts(dens, mask):
    def upper(i):
        return masked_lanes(dens, mask, i, 0, upper_width(i))

    def lower(i):
        return masked_lanes(dens, mask, i, WIDE - lower_width(i), WIDE)

    return lower, upper


def chosen(pick, first, second):
    def get(n, lo, hi):
        return jnp.where(pick, first[n, :, lo:hi], second[n, :, lo:hi])

    return get


def sent_upper(buf):
    def get(i):
        if i == 0:
            return jnp.concatenate([buf(0, 0, HALF), buf(1, 0, HALF)], axis=1)
        if i < 8:
            rest = HALF - 128 * (i // 2)
            return jnp.concatenate([buf(1 + i, 0, HALF), buf(9 + i, 0, rest)], axis=1)
        return buf(9 + ROWS - i if i > 8 else 9, 0, HALF)

    return get


def sent_lower(buf):
    def get(i):
        pieces = [buf(n, lane, lane + lanes) for n, lane, _, lanes in lower_place(i)]
        return pieces[0] if len(pieces) == 1 else jnp.concatenate(pieces, axis=1)

    return get


def build(dst, base, lower, upper, packed=False):
    lane = lax.broadcasted_iota(jnp.int32, (BS, WIDE), 1)
    for i in range(ROWS):
        rows = slice(base + i * BS, base + (i + 1) * BS)
        parts = []
        if i > 0:
            parts.append(lower(i) if lower else jnp.zeros((BS, lower_width(i)), jnp.bfloat16))
        placed = packed and i >= 8
        if upper and not placed:
            parts.append(upper(i))
        else:
            parts.append(jnp.zeros((BS, upper_width(i)), jnp.bfloat16))
        both = jnp.concatenate(parts, axis=1) if i > 0 else parts[0]
        if i % 2:
            both = both[:, BS : BS + WIDE]
            if not lower:
                both = jnp.where(lane >= i * BS, both, jnp.zeros_like(both))
            if not upper or placed:
                both = jnp.where(lane < i * BS, both, jnp.zeros_like(both))
        if placed:
            dst[rows, :HALF] = both[:, :HALF]
            right = jnp.where(lane[:, HALF:] >= i * BS, upper(i), both[:, HALF:])
            dst[rows, HALF:] = right
        else:
            dst[rows, :] = both


def mirror(dst, base):
    r = lax.broadcasted_iota(jnp.int32, (TILE, TILE), 0)
    c = lax.broadcasted_iota(jnp.int32, (TILE, TILE), 1)
    eye = jnp.where(r == c, 1.0, 0.0).astype(jnp.bfloat16)
    above = lax.shift_right_logical(r, 6) < lax.shift_right_logical(c, 6)
    strict = jnp.where(above, 1.0, 0.0).astype(jnp.bfloat16)
    for n in range(WIDE // TILE):
        rows = slice(base + n * TILE, base + (n + 1) * TILE)
        cols = slice(n * TILE, (n + 1) * TILE)
        diag = dst[rows, cols]
        dst[rows, cols] = diag + dot(eye, diag * strict, NT).astype(jnp.bfloat16)
        for m in range(n + 1, WIDE // TILE):
            tile = dst[rows, m * TILE : (m + 1) * TILE]
            turned = dot(eye, tile, NT).astype(jnp.bfloat16)
            dst[base + m * TILE : base + (m + 1) * TILE, cols] = turned


def prepare_kernel(dens, pat, y, mask):
    q = lax.axis_index("depth")

    @pl.when((q == 0) | (q == 2))
    def _():
        mask[...] = expand(pat[...], WIDE)
        build(y, 0, None, own_parts(dens, mask)[1])

    @pl.when(q == 2)
    def _():
        mirror(y, 0)


def main_kernel(
    groups, dens, pat, y, got_a1, got_a2, got_b1, got_b2, own, first1, second1, first2, second2, mask, z
):
    q = lax.axis_index("depth")
    late = late_half(groups // 2)
    group = group_index()
    turn = (group == groups - 1) | (group == groups // 2 - 1)
    next_late = late != turn
    mask[...] = expand(pat[...], WIDE)
    own_lower, own_upper = own_parts(dens, mask)

    def finish(static_q, tile_row, window):
        for n in range(TILE // BS):
            i = tile_row * (TILE // BS) + n
            row = window[n * BS : (n + 1) * BS, n * BS : n * BS + WIDE].astype(jnp.bfloat16)

            def share(p):
                p = p % 4
                return row[:, p * TILE : (p + 1) * TILE]

            own[i] = share(static_q)
            first2[i] = jnp.where(late, share(static_q - 1), share(static_q + 1))
            second2[i] = jnp.where(late, share(static_q + 1), share(static_q - 1))
            if i < 8:
                first1[i] = share(static_q + 2)
            else:
                second1[i - 8] = share(static_q + 2)

    def products(static_q):
        for t in range(WIDE // TILE):
            lo, hi = t * TILE, (t + 1) * TILE
            depth_hi = hi if static_q == 3 else WIDE
            window = dot(z[lo:hi, :depth_hi], z[lo : lo + WIDE + TILE, :depth_hi], NT)
            if static_q == 0:
                first = dot(y[lo:hi, lo:], y[lo:, lo:], NT)
                window = jnp.concatenate(
                    [window[:, : WIDE - lo] + first, window[:, WIDE - lo :]], axis=1
                )
            if static_q == 2:
                first = dot(y[lo:hi, :], y[lo:, :], NT)
                second = dot(y[lo:hi, :], z[:WIDE, :hi], NN)
                window = window + jnp.concatenate([first, second], axis=1)
            finish(static_q, t, window)

    @pl.when(q == 0)
    def _():
        build(z, 0, own_lower, sent_upper(chosen(late, got_a1, got_a2)), True)
        build(z, WIDE, None, sent_upper(chosen(late, got_a2, got_a1)), True)
        products(0)

    @pl.when(q == 1)
    def _():
        for ref in (own, first1, second1, first2, second2):
            ref[...] = jnp.zeros_like(ref)

    @pl.when(q == 2)
    def _():
        build(z, 0, own_lower, sent_upper(chosen(late, got_a1, got_a2)), True)
        build(z, WIDE, None, sent_upper(chosen(next_late, got_b1, got_b2)), True)
        mirror(z, WIDE)
        products(2)

    @pl.when(q == 3)
    def _():
        build(z, 0, own_lower, None)
        lower = sent_lower(chosen(next_late, got_b2, got_b1))
        build(z, WIDE, lower, sent_upper(chosen(next_late, got_a2, got_a1)), True)
        products(3)


def add_kernel(first, second, got_first, got_second, first_out, second_out):
    for i in range(8):
        total = first[i].astype(jnp.float32) + got_first[i].astype(jnp.float32)
        first_out[i] = total.astype(jnp.bfloat16)
        second_out[i] = second[i]
        total = second[8 + i].astype(jnp.float32) + got_second[i].astype(jnp.float32)
        second_out[8 + i] = total.astype(jnp.bfloat16)
        first_out[8 + i] = first[8 + i]


def final_kernel(own, got_first, got_second, keep, out, mask):
    mask[...] = expand(keep[...], TILE)
    for i in range(ROWS):
        total = own[i].astype(jnp.float32) + got_first[i].astype(jnp.float32)
        total = total + got_second[i].astype(jnp.float32)
        out[i] = (total * mask[i : i + 1, :]).astype(jnp.bfloat16)


def vmem(count):
    return [pl.BlockSpec(memory_space=pltpu.VMEM)] * count


def per_device(groups, density, pattern, keep_filter):
    mib = 1024 * 1024

    def call(kernel, outs, scratch, limit, flops, moved, *operands):
        return pl.pallas_call(
            kernel,
            out_shape=tuple(jax.ShapeDtypeStruct(shape, jnp.bfloat16) for shape in outs),
            in_specs=vmem(len(operands)),
            out_specs=tuple(vmem(len(outs))),
            scratch_shapes=scratch,
            compiler_params=pltpu.CompilerParams(vmem_limit_bytes=limit * mib),
            cost_estimate=pl.CostEstimate(flops=flops, bytes_accessed=moved, transcendentals=0),
        )(*operands)

    packed = (17, BS, HALF)
    share = (ROWS, BS, TILE)
    half_share = (ROWS // 2, BS, TILE)
    slot_mask = pltpu.VMEM((ROWS, WIDE), jnp.float32)

    half = groups // 2
    send_1, send_2 = call(
        functools.partial(pack_kernel, half),
        (packed,) * 2,
        [slot_mask],
        24,
        4_000_000,
        5_500_000,
        density,
        pattern,
    )

    def device(g, q):
        return (g % groups) * 4 + q

    routes_a, routes_b = ([], []), ([], [])
    for g in range(groups):
        late = int(g >= half)
        routes_a[1 - late].extend([(device(g, 1), device(g, 0)), (device(g, 3), device(g, 2))])
        routes_a[late].append((device(g, 3), device(g - 1, 3)))
        routes_a[int((g - 1) % groups >= half)].append((device(g, 0), device(g - 1, 0)))
        routes_b[late].append((device(g, 2), device(g - 1, 3)))
        routes_b[1 - late].append((device(g, 2), device(g - 1, 2)))
    got = [
        lax.ppermute(send_1, AXES, routes_a[0]),
        lax.ppermute(send_1, AXES, routes_b[0]),
        lax.ppermute(send_1, AXES, routes_a[1]),
        lax.ppermute(send_2, AXES, routes_b[1]),
    ]
    got = [got[0], got[2], got[1], got[3]]

    (prepared,) = call(
        prepare_kernel, ((WIDE, WIDE),), [slot_mask], 24, 1_000_000_000, 4_500_000, density, pattern
    )
    own, first1, second1, first2, second2 = call(
        functools.partial(main_kernel, groups),
        (share, half_share, half_share, share, share),
        [slot_mask, pltpu.VMEM((2 * WIDE, WIDE), jnp.bfloat16)],
        40,
        8_000_000_000,
        10_000_000,
        density,
        pattern,
        prepared,
        *got,
    )

    first_route, second_route = [], []
    for g in range(groups):
        for q in range(4):
            up = (device(g, q), device(g, (q + 1) % 4))
            down = (device(g, q), device(g, (q - 1) % 4))
            first_route.append(down if g >= half else up)
            second_route.append(up if g >= half else down)
    got_first = lax.ppermute(first1, AXES, first_route)
    got_second = lax.ppermute(second1, AXES, second_route)
    first2, second2 = call(
        add_kernel,
        (share,) * 2,
        [],
        16,
        1_000_000,
        3_000_000,
        first2,
        second2,
        got_first,
        got_second,
    )
    got_first = lax.ppermute(first2, AXES, first_route)
    got_second = lax.ppermute(second2, AXES, second_route)
    (out,) = call(
        final_kernel,
        (share,),
        [pltpu.VMEM((ROWS, TILE), jnp.float32)],
        16,
        1_500_000,
        2_700_000,
        own,
        got_first,
        got_second,
        keep_filter,
    )
    return out


def solution(mesh):
    placed = (
        P(("row", "col"), None, "depth"),
        P(("row", "col"), "depth"),
        P(("row", "col"), "depth"),
    )
    groups = mesh.shape["row"] * mesh.shape["col"]
    return jax.shard_map(
        functools.partial(per_device, groups),
        mesh=mesh,
        in_specs=placed,
        out_specs=P(("row", "col"), None, "depth"),
        check_vma=False,
    )
```

```python
import functools
import jax
import jax.numpy as jnp
from jax import lax
from jax.experimental import pallas as pl
from jax.experimental.pallas import tpu as pltpu
from jax.sharding import PartitionSpec as P

BS = 64
ROWS = 16
WIDE = ROWS * BS
HALF = WIDE // 2
TILE = 256
AXES = ("row", "col", "depth")
NT = (((1,), (1,)), ((), ()))
NN = (((1,), (0,)), ((), ()))


def dot(a, b, dims):
    return lax.dot_general(a, b, dims, preferred_element_type=jnp.float32)


def expand(flags, cols):
    count = flags.shape[1]
    slot = lax.broadcasted_iota(jnp.int32, (count, cols), 0)
    col = lax.broadcasted_iota(jnp.int32, (count, cols), 1)
    spread = jnp.where((col >= slot * BS) & (col < slot * BS + BS), 1.0, 0.0)
    return dot(flags.astype(jnp.float32), spread, NN)


def masked_lanes(dens, mask, i, lo, hi):
    m = jnp.broadcast_to(mask[i : i + 1, lo:hi], (16, hi - lo)).astype(jnp.bfloat16)
    x = dens[i, :, lo:hi].reshape(BS // 16, 16, hi - lo)
    return (x * m[None]).reshape(BS, hi - lo)


def group_index():
    return lax.axis_index("row") * lax.axis_size("col") + lax.axis_index("col")


def late_half(groups_half):
    return group_index() >= groups_half


def upper_width(i):
    return WIDE - 128 * (i // 2)


def lower_width(i):
    return 128 * ((i - 1) // 2 + 1)


def lower_place(i):
    a, e = (i - 1) // 2, (i - 1) % 2
    width = lower_width(i)
    if a < 3:
        return [(2 * (2 * a + e) + 1, HALF - width, 0, width)]
    if a == 3:
        return [(12 + e, 0, 0, width)]
    row = 7 if i == ROWS - 1 else 2 * (6 - a) + e
    return [(2 * row, 0, 0, HALF), (2 * row + 1, 0, HALF, width - HALF)]


def put_upper(own, put):
    put(0, own(0, 0, HALF))
    put(1, own(0, HALF, WIDE))
    for i in range(1, 9):
        put(1 + i, own(i, 0, HALF))
    for i in range(1, 8):
        left = own(i, HALF, WIDE - 128 * (i // 2))[:, : HALF - BS * i]
        right = own(ROWS - i, 0, 128 * ((i + 1) // 2))[:, : BS * i]
        put(9 + i, jnp.concatenate([left, right], axis=1))


def pack(groups_half, dens, mask, send, lower_if_late):
    late = late_half(groups_half)
    send_lower = (lax.axis_index("depth") == 2) & (late == lower_if_late)

    def own(i, lo, hi):
        return masked_lanes(dens, mask, i, lo, hi)

    def put(n, part):
        send[n] = part

    @pl.when(jnp.logical_not(send_lower))
    def _():
        put_upper(own, put)

    @pl.when(send_lower)
    def _():
        for i in range(1, ROWS):
            width = lower_width(i)
            part = own(i, WIDE - width, WIDE)
            for n, lane, first, lanes in lower_place(i):
                send[n, :, lane : lane + lanes] = part[:, first : first + lanes]
        send[16] = jnp.zeros((BS, HALF), jnp.bfloat16)


def pack_kernel(groups_half, dens, pat, send, mask):
    mask[...] = expand(pat[...], WIDE)
    pack(groups_half, dens, mask, send, True)


def pack_first_kernel(groups_half, dens, mask, send):
    pack(groups_half, dens, mask, send, False)


def own_parts(dens, mask):
    def upper(i):
        return masked_lanes(dens, mask, i, 0, upper_width(i))

    def lower(i):
        return masked_lanes(dens, mask, i, WIDE - lower_width(i), WIDE)

    return lower, upper


def chosen(pick, first, second):
    def get(n, lo, hi):
        return jnp.where(pick, first[n, :, lo:hi], second[n, :, lo:hi])

    return get


def sent_upper(buf):
    def get(i):
        if i == 0:
            return jnp.concatenate([buf(0, 0, HALF), buf(1, 0, HALF)], axis=1)
        if i < 8:
            rest = HALF - 128 * (i // 2)
            return jnp.concatenate([buf(1 + i, 0, HALF), buf(9 + i, 0, rest)], axis=1)
        return buf(9 + ROWS - i if i > 8 else 9, 0, HALF)

    return get


def sent_lower(buf):
    def get(i):
        pieces = [buf(n, lane, lane + lanes) for n, lane, _, lanes in lower_place(i)]
        return pieces[0] if len(pieces) == 1 else jnp.concatenate(pieces, axis=1)

    return get


def build(dst, base, lower, upper, packed=False):
    lane = lax.broadcasted_iota(jnp.int32, (BS, WIDE), 1)
    for i in range(ROWS):
        rows = slice(base + i * BS, base + (i + 1) * BS)
        parts = []
        if i > 0:
            parts.append(lower(i) if lower else jnp.zeros((BS, lower_width(i)), jnp.bfloat16))
        placed = packed and i >= 8
        if upper and not placed:
            parts.append(upper(i))
        else:
            parts.append(jnp.zeros((BS, upper_width(i)), jnp.bfloat16))
        both = jnp.concatenate(parts, axis=1) if i > 0 else parts[0]
        if i % 2:
            both = both[:, BS : BS + WIDE]
            if not lower:
                both = jnp.where(lane >= i * BS, both, jnp.zeros_like(both))
            if not upper or placed:
                both = jnp.where(lane < i * BS, both, jnp.zeros_like(both))
        if placed:
            dst[rows, :HALF] = both[:, :HALF]
            right = jnp.where(lane[:, HALF:] >= i * BS, upper(i), both[:, HALF:])
            dst[rows, HALF:] = right
        else:
            dst[rows, :] = both


def mirror(dst, base):
    r = lax.broadcasted_iota(jnp.int32, (TILE, TILE), 0)
    c = lax.broadcasted_iota(jnp.int32, (TILE, TILE), 1)
    eye = jnp.where(r == c, 1.0, 0.0).astype(jnp.bfloat16)
    above = lax.shift_right_logical(r, 6) < lax.shift_right_logical(c, 6)
    strict = jnp.where(above, 1.0, 0.0).astype(jnp.bfloat16)
    for n in range(WIDE // TILE):
        rows = slice(base + n * TILE, base + (n + 1) * TILE)
        cols = slice(n * TILE, (n + 1) * TILE)
        diag = dst[rows, cols]
        dst[rows, cols] = diag + dot(eye, diag * strict, NT).astype(jnp.bfloat16)
        for m in range(n + 1, WIDE // TILE):
            tile = dst[rows, m * TILE : (m + 1) * TILE]
            turned = dot(eye, tile, NT).astype(jnp.bfloat16)
            dst[base + m * TILE : base + (m + 1) * TILE, cols] = turned


def prepare_kernel(dens, mask, y, acc):
    q = lax.axis_index("depth")
    own_lower, own_upper = own_parts(dens, mask)

    @pl.when((q == 0) | (q == 2))
    def _():
        build(y, 0, None, own_upper)

    @pl.when(q == 2)
    def _():
        mirror(y, 0)

    @pl.when(q == 3)
    def _():
        build(y, 0, own_lower, None)

    @pl.when(q != 1)
    def _():
        for t in range(WIDE // TILE):
            lo, hi = t * TILE, (t + 1) * TILE
            acc[t, :, : WIDE - lo] = dot(y[lo:hi, :], y[lo:, :], NT)


def main_kernel(
    groups, dens, mask, y, acc, got_a1, got_a2, got_b1, got_b2, own, first1, second1, first2, second2, z
):
    q = lax.axis_index("depth")
    late = late_half(groups // 2)
    group = group_index()
    turn = (group == groups - 1) | (group == groups // 2 - 1)
    next_late = late != turn
    own_lower, own_upper = own_parts(dens, mask)

    def finish(static_q, tile_row, window):
        for n in range(TILE // BS):
            i = tile_row * (TILE // BS) + n
            row = window[n * BS : (n + 1) * BS, n * BS : n * BS + WIDE].astype(jnp.bfloat16)

            def share(p):
                p = p % 4
                return row[:, p * TILE : (p + 1) * TILE]

            own[i] = share(static_q)
            first2[i] = jnp.where(late, share(static_q - 1), share(static_q + 1))
            second2[i] = jnp.where(late, share(static_q + 1), share(static_q - 1))
            if i < 8:
                first1[i] = share(static_q + 2)
            else:
                second1[i - 8] = share(static_q + 2)

    def products(static_q):
        for t in range(WIDE // TILE):
            lo, hi = t * TILE, (t + 1) * TILE
            ahead = acc[t, :, : WIDE - lo]
            if static_q == 3:
                later = dot(y[lo:hi, :hi], z[WIDE : WIDE + hi, :hi], NT)
                window = jnp.concatenate([ahead, later], axis=1)
            else:
                window = dot(z[lo:hi, :], z[lo : lo + WIDE + TILE, :], NT)
                later = window[:, WIDE - lo :]
                if static_q == 2:
                    later = later + dot(y[lo:hi, :], z[:WIDE, :hi], NN)
                window = jnp.concatenate([window[:, : WIDE - lo] + ahead, later], axis=1)
            finish(static_q, t, window)

    @pl.when(q == 0)
    def _():
        build(z, 0, own_lower, sent_upper(chosen(late, got_a1, got_a2)), True)
        build(z, WIDE, None, sent_upper(chosen(late, got_a2, got_a1)), True)
        products(0)

    @pl.when(q == 1)
    def _():
        for ref in (own, first1, second1, first2, second2):
            ref[...] = jnp.zeros_like(ref)

    @pl.when(q == 2)
    def _():
        build(z, 0, own_lower, sent_upper(chosen(late, got_a1, got_a2)), True)
        build(z, WIDE, None, sent_upper(chosen(next_late, got_b1, got_b2)), True)
        mirror(z, WIDE)
        products(2)

    @pl.when(q == 3)
    def _():
        lower = sent_lower(chosen(next_late, got_b2, got_b1))
        build(z, WIDE, lower, sent_upper(chosen(next_late, got_a2, got_a1)), True)
        products(3)


def add_kernel(first, second, got_first, got_second, first_out, second_out):
    for i in range(8):
        total = first[i].astype(jnp.float32) + got_first[i].astype(jnp.float32)
        first_out[i] = total.astype(jnp.bfloat16)
        second_out[i] = second[i]
        total = second[8 + i].astype(jnp.float32) + got_second[i].astype(jnp.float32)
        second_out[8 + i] = total.astype(jnp.bfloat16)
        first_out[8 + i] = first[8 + i]


def final_kernel(own, got_first, got_second, keep, out, mask):
    mask[...] = expand(keep[...], TILE)
    for i in range(ROWS):
        total = own[i].astype(jnp.float32) + got_first[i].astype(jnp.float32)
        total = total + got_second[i].astype(jnp.float32)
        out[i] = (total * mask[i : i + 1, :]).astype(jnp.bfloat16)


def vmem(count):
    return [pl.BlockSpec(memory_space=pltpu.VMEM)] * count


def per_device(groups, density, pattern, keep_filter):
    mib = 1024 * 1024
    window_rows = (WIDE // TILE, TILE, WIDE)
    slot_mask = (ROWS, WIDE)
    wide_types = (window_rows, slot_mask)

    def call(kernel, outs, scratch, limit, flops, moved, *operands):
        return pl.pallas_call(
            kernel,
            out_shape=tuple(
                jax.ShapeDtypeStruct(shape, jnp.float32 if shape in wide_types else jnp.bfloat16)
                for shape in outs
            ),
            in_specs=vmem(len(operands)),
            out_specs=tuple(vmem(len(outs))),
            scratch_shapes=scratch,
            compiler_params=pltpu.CompilerParams(vmem_limit_bytes=limit * mib),
            cost_estimate=pl.CostEstimate(flops=flops, bytes_accessed=moved, transcendentals=0),
        )(*operands)

    packed = (17, BS, HALF)
    share = (ROWS, BS, TILE)
    half_share = (ROWS // 2, BS, TILE)

    half = groups // 2
    send_2, mask = call(
        functools.partial(pack_kernel, half),
        (packed, slot_mask),
        [],
        16,
        4_000_000,
        3_500_000,
        density,
        pattern,
    )
    (send_1,) = call(
        functools.partial(pack_first_kernel, half),
        (packed,),
        [],
        16,
        4_000_000,
        3_500_000,
        density,
        mask,
    )
    prepared, ahead = call(
        prepare_kernel,
        ((WIDE, WIDE), window_rows),
        [],
        16,
        3_000_000_000,
        9_500_000,
        density,
        mask,
    )

    def device(g, q):
        return (g % groups) * 4 + q

    routes_a, routes_b = ([], []), ([], [])
    for g in range(groups):
        late = int(g >= half)
        routes_a[1 - late].extend([(device(g, 1), device(g, 0)), (device(g, 3), device(g, 2))])
        routes_a[late].append((device(g, 3), device(g - 1, 3)))
        routes_a[int((g - 1) % groups >= half)].append((device(g, 0), device(g - 1, 0)))
        routes_b[late].append((device(g, 2), device(g - 1, 3)))
        routes_b[1 - late].append((device(g, 2), device(g - 1, 2)))
    got_a1 = lax.ppermute(send_1, AXES, routes_a[0])
    got_b1 = lax.ppermute(send_1, AXES, routes_b[0])
    got_a2 = lax.ppermute(send_2, AXES, routes_a[1])
    got_b2 = lax.ppermute(send_2, AXES, routes_b[1])

    own, first1, second1, first2, second2 = call(
        functools.partial(main_kernel, groups),
        (share, half_share, half_share, share, share),
        [pltpu.VMEM((2 * WIDE, WIDE), jnp.bfloat16)],
        20,
        6_000_000_000,
        14_000_000,
        density,
        mask,
        prepared,
        ahead,
        got_a1,
        got_a2,
        got_b1,
        got_b2,
    )

    first_route, second_route = [], []
    for g in range(groups):
        for q in range(4):
            up = (device(g, q), device(g, (q + 1) % 4))
            down = (device(g, q), device(g, (q - 1) % 4))
            first_route.append(down if g >= half else up)
            second_route.append(up if g >= half else down)
    got_first = lax.ppermute(first1, AXES, [r for r in first_route if r[0] % 4 != 1])
    got_second = lax.ppermute(second1, AXES, [r for r in second_route if r[0] % 4 != 1])
    first2, second2 = call(
        add_kernel,
        (share,) * 2,
        [],
        16,
        1_000_000,
        3_000_000,
        first2,
        second2,
        got_first,
        got_second,
    )
    got_first = lax.ppermute(first2, AXES, first_route)
    got_second = lax.ppermute(second2, AXES, second_route)
    (out,) = call(
        final_kernel,
        (share,),
        [pltpu.VMEM((ROWS, TILE), jnp.float32)],
        16,
        1_500_000,
        2_700_000,
        own,
        got_first,
        got_second,
        keep_filter,
    )
    return out


def solution(mesh):
    placed = (
        P(("row", "col"), None, "depth"),
        P(("row", "col"), "depth"),
        P(("row", "col"), "depth"),
    )
    groups = mesh.shape["row"] * mesh.shape["col"]
    return jax.shard_map(
        functools.partial(per_device, groups),
        mesh=mesh,
        in_specs=placed,
        out_specs=P(("row", "col"), None, "depth"),
        check_vma=False,
    )
```

```python
import functools
import jax
import jax.numpy as jnp
from jax import lax
from jax.experimental import pallas as pl
from jax.experimental.pallas import tpu as pltpu
from jax.sharding import PartitionSpec as P

BS = 64
ROWS = 16
WIDE = ROWS * BS
HALF = WIDE // 2
TILE = 256
AXES = ("row", "col", "depth")
NT = (((1,), (1,)), ((), ()))
NN = (((1,), (0,)), ((), ()))


def dot(a, b, dims):
    return lax.dot_general(a, b, dims, preferred_element_type=jnp.float32)


def expand(flags, cols):
    count = flags.shape[1]
    slot = lax.broadcasted_iota(jnp.int32, (count, cols), 0)
    col = lax.broadcasted_iota(jnp.int32, (count, cols), 1)
    spread = jnp.where((col >= slot * BS) & (col < slot * BS + BS), 1.0, 0.0)
    return dot(flags.astype(jnp.float32), spread, NN)


def masked_lanes(dens, mask, i, lo, hi):
    m = jnp.broadcast_to(mask[i : i + 1, lo:hi], (16, hi - lo)).astype(jnp.bfloat16)
    x = dens[i, :, lo:hi].reshape(BS // 16, 16, hi - lo)
    return (x * m[None]).reshape(BS, hi - lo)


def late_half(groups_half):
    group = lax.axis_index("row") * lax.axis_size("col") + lax.axis_index("col")
    return group >= groups_half


def upper_width(i):
    return WIDE - 128 * (i // 2)


def lower_width(i):
    return 128 * ((i - 1) // 2 + 1)


def lower_place(i):
    a, e = (i - 1) // 2, (i - 1) % 2
    width = lower_width(i)
    if a < 3:
        return [(2 * (2 * a + e) + 1, HALF - width, 0, width)]
    if a == 3:
        return [(12 + e, 0, 0, width)]
    row = 7 if i == ROWS - 1 else 2 * (6 - a) + e
    return [(2 * row, 0, 0, HALF), (2 * row + 1, 0, HALF, width - HALF)]


def put_upper(own, put):
    put(0, own(0, 0, HALF))
    put(1, own(0, HALF, WIDE))
    for i in range(1, 9):
        put(1 + i, own(i, 0, HALF))
    for i in range(1, 8):
        left = own(i, HALF, WIDE - 128 * (i // 2))[:, : HALF - BS * i]
        right = own(ROWS - i, 0, 128 * ((i + 1) // 2))[:, : BS * i]
        put(9 + i, jnp.concatenate([left, right], axis=1))


def put_lower(own, put):
    for i in range(1, ROWS):
        width = lower_width(i)
        part = own(i, WIDE - width, WIDE)
        for n, lane, first, lanes in lower_place(i):
            put(n, lane, part[:, first : first + lanes])


def pack_kernel(dens, pat, upper, diag, mask):
    mask[...] = expand(pat[...], WIDE)

    def own(i, lo, hi):
        return masked_lanes(dens, mask, i, lo, hi)

    def put(n, part):
        upper[n] = part

    put_upper(own, put)
    for a in range(ROWS // 2):
        pair = [own(2 * a + e, 0, 2 * BS)[:, :BS] for e in range(2)]
        diag[a] = jnp.concatenate(pair, axis=1)


def pack_first_kernel(dens, mask, upper, lower):
    def own(i, lo, hi):
        return masked_lanes(dens, mask, i, lo, hi)

    def put(n, part):
        upper[n] = part

    def put_at(n, lane, part):
        lower[n, :, lane : lane + part.shape[1]] = part

    put_upper(own, put)
    put_lower(own, put_at)


def own_parts(dens, mask):
    def upper(i):
        return masked_lanes(dens, mask, i, 0, upper_width(i))

    def lower(i):
        return masked_lanes(dens, mask, i, WIDE - lower_width(i), WIDE)

    return lower, upper


def sent_upper(buf):
    def get(i):
        if i == 0:
            return jnp.concatenate([buf[0], buf[1]], axis=1)
        if i < 8:
            rest = HALF - 128 * (i // 2)
            return jnp.concatenate([buf[1 + i], buf[9 + i, :, :rest]], axis=1)
        return buf[9 + ROWS - i if i > 8 else 9]

    return get


def sent_lower(buf):
    def get(i):
        pieces = [buf[n, :, lane : lane + lanes] for n, lane, _, lanes in lower_place(i)]
        return pieces[0] if len(pieces) == 1 else jnp.concatenate(pieces, axis=1)

    return get


def build(dst, base, lower, upper, packed=False):
    lane = lax.broadcasted_iota(jnp.int32, (BS, WIDE), 1)
    for i in range(ROWS):
        rows = slice(base + i * BS, base + (i + 1) * BS)
        parts = []
        if i > 0:
            parts.append(lower(i) if lower else jnp.zeros((BS, lower_width(i)), jnp.bfloat16))
        placed = packed and i >= 8
        if upper and not placed:
            parts.append(upper(i))
        else:
            parts.append(jnp.zeros((BS, upper_width(i)), jnp.bfloat16))
        both = jnp.concatenate(parts, axis=1) if i > 0 else parts[0]
        if i % 2:
            both = both[:, BS : BS + WIDE]
            if not lower:
                both = jnp.where(lane >= i * BS, both, jnp.zeros_like(both))
            if not upper or placed:
                both = jnp.where(lane < i * BS, both, jnp.zeros_like(both))
        if placed:
            dst[rows, :HALF] = both[:, :HALF]
            right = jnp.where(lane[:, HALF:] >= i * BS, upper(i), both[:, HALF:])
            dst[rows, HALF:] = right
        else:
            dst[rows, :] = both


def put_diagonal(dst, base, diag):
    lane = lax.broadcasted_iota(jnp.int32, (BS, 2 * BS), 1)
    for i in range(ROWS):
        a = i // 2
        at = (slice(base + i * BS, base + (i + 1) * BS), slice(2 * BS * a, 2 * BS * (a + 1)))
        mine = lane >= BS if i % 2 else lane < BS
        dst[at] = jnp.where(mine, diag[a], dst[at])


def mirror(dst, base, from_lower=False):
    r = lax.broadcasted_iota(jnp.int32, (TILE, TILE), 0)
    c = lax.broadcasted_iota(jnp.int32, (TILE, TILE), 1)
    eye = jnp.where(r == c, 1.0, 0.0).astype(jnp.bfloat16)
    block_r, block_c = lax.shift_right_logical(r, 6), lax.shift_right_logical(c, 6)
    given = block_r > block_c if from_lower else block_r < block_c
    strict = jnp.where(given, 1.0, 0.0).astype(jnp.bfloat16)

    def tile_at(n, m):
        return (slice(base + n * TILE, base + (n + 1) * TILE), slice(m * TILE, (m + 1) * TILE))

    for n in range(WIDE // TILE):
        diag = dst[tile_at(n, n)]
        dst[tile_at(n, n)] = diag + dot(eye, diag * strict, NT).astype(jnp.bfloat16)
        for m in range(n + 1, WIDE // TILE):
            source, target = (tile_at(m, n), tile_at(n, m))
            if not from_lower:
                source, target = target, source
            dst[target] = dot(eye, dst[source], NT).astype(jnp.bfloat16)


def prepare_kernel(dens, mask, y, acc):
    q = lax.axis_index("depth")
    own_lower, own_upper = own_parts(dens, mask)

    @pl.when((q == 0) | (q == 2))
    def _():
        build(y, 0, None, own_upper)

    @pl.when(q == 2)
    def _():
        mirror(y, 0)

    @pl.when(q == 3)
    def _():
        build(y, 0, own_lower, None)

    @pl.when(q != 1)
    def _():
        for t in range(WIDE // TILE):
            lo, hi = t * TILE, (t + 1) * TILE
            acc[t, :, : WIDE - lo] = dot(y[lo:hi, :], y[lo:, :], NT)


def main_kernel(
    groups_half,
    dens,
    mask,
    y,
    acc,
    got_depth,
    got_y,
    got_lower,
    got_diag,
    own,
    first1,
    second1,
    first_free,
    second_free,
    first_due,
    second_due,
    z,
):
    q = lax.axis_index("depth")
    late = late_half(groups_half)
    own_lower, own_upper = own_parts(dens, mask)

    def finish(static_q, tile_row, window):
        for n in range(TILE // BS):
            i = tile_row * (TILE // BS) + n
            row = window[n * BS : (n + 1) * BS, n * BS : n * BS + WIDE].astype(jnp.bfloat16)

            def share(p):
                p = p % 4
                return row[:, p * TILE : (p + 1) * TILE]

            own[i] = share(static_q)
            first = jnp.where(late, share(static_q - 1), share(static_q + 1))
            second = jnp.where(late, share(static_q + 1), share(static_q - 1))
            if i < 8:
                first1[i] = share(static_q + 2)
                first_due[i] = first
                second_free[i] = second
            else:
                second1[i - 8] = share(static_q + 2)
                first_free[i - 8] = first
                second_due[i - 8] = second

    def products(static_q):
        for t in range(WIDE // TILE):
            lo, hi = t * TILE, (t + 1) * TILE
            ahead = acc[t, :, : WIDE - lo]
            if static_q == 3:
                later = dot(y[lo:hi, :hi], z[WIDE : WIDE + hi, :hi], NT)
                window = jnp.concatenate([ahead, later], axis=1)
            else:
                window = dot(z[lo:hi, :], z[lo : lo + WIDE + TILE, :], NT)
                later = window[:, WIDE - lo :]
                if static_q == 2:
                    later = later + dot(y[lo:hi, :], z[:WIDE, :hi], NN)
                window = jnp.concatenate([window[:, : WIDE - lo] + ahead, later], axis=1)
            finish(static_q, t, window)

    @pl.when(q == 0)
    def _():
        build(z, 0, own_lower, sent_upper(got_depth), True)
        build(z, WIDE, None, sent_upper(got_y), True)
        products(0)

    @pl.when(q == 1)
    def _():
        for ref in (own, first_free, second_free, first_due, second_due):
            ref[...] = jnp.zeros_like(ref)

    @pl.when(q == 2)
    def _():
        build(z, 0, own_lower, sent_upper(got_depth), True)
        build(z, WIDE, sent_lower(got_lower), None)
        put_diagonal(z, WIDE, got_diag)
        mirror(z, WIDE, True)
        products(2)

    @pl.when(q == 3)
    def _():
        build(z, WIDE, sent_lower(got_lower), sent_upper(got_y), True)
        products(3)


def add_kernel(first, second, got_first, got_second, first_out, second_out):
    for i in range(8):
        total = first[i].astype(jnp.float32) + got_first[i].astype(jnp.float32)
        first_out[i] = total.astype(jnp.bfloat16)
        total = second[i].astype(jnp.float32) + got_second[i].astype(jnp.float32)
        second_out[i] = total.astype(jnp.bfloat16)


def final_kernel(own, first_free, second_free, first_due, second_due, keep, out, mask):
    mask[...] = expand(keep[...], TILE)
    for i in range(ROWS):
        one, other = (first_due, second_free) if i < 8 else (first_free, second_due)
        total = own[i].astype(jnp.float32) + one[i % 8].astype(jnp.float32)
        total = total + other[i % 8].astype(jnp.float32)
        out[i] = (total * mask[i : i + 1, :]).astype(jnp.bfloat16)


def vmem(count):
    return [pl.BlockSpec(memory_space=pltpu.VMEM)] * count


def per_device(groups, density, pattern, keep_filter):
    mib = 1024 * 1024
    window_rows = (WIDE // TILE, TILE, WIDE)
    slot_mask = (ROWS, WIDE)
    wide_types = (window_rows, slot_mask)

    def call(kernel, outs, scratch, limit, flops, moved, *operands):
        return pl.pallas_call(
            kernel,
            out_shape=tuple(
                jax.ShapeDtypeStruct(shape, jnp.float32 if shape in wide_types else jnp.bfloat16)
                for shape in outs
            ),
            in_specs=vmem(len(operands)),
            out_specs=tuple(vmem(len(outs))),
            scratch_shapes=scratch,
            compiler_params=pltpu.CompilerParams(vmem_limit_bytes=limit * mib),
            cost_estimate=pl.CostEstimate(flops=flops, bytes_accessed=moved, transcendentals=0),
        )(*operands)

    upper_part = (17, BS, HALF)
    lower_part = (16, BS, HALF)
    share = (ROWS, BS, TILE)
    half_share = (ROWS // 2, BS, TILE)
    half = groups // 2

    upper, diag, mask = call(
        pack_kernel,
        (upper_part, (ROWS // 2, BS, 2 * BS), slot_mask),
        [],
        16,
        4_000_000,
        3_500_000,
        density,
        pattern,
    )
    upper_first, lower = call(
        pack_first_kernel,
        (upper_part, lower_part),
        [],
        16,
        4_000_000,
        4_500_000,
        density,
        mask,
    )
    prepared, ahead = call(
        prepare_kernel,
        ((WIDE, WIDE), window_rows),
        [],
        16,
        3_000_000_000,
        9_500_000,
        density,
        mask,
    )

    def device(g, q):
        return (g % groups) * 4 + q

    by_depth, by_y, of_lower, of_diag, first_route, second_route = [], [], [], [], [], []
    for g in range(groups):
        by_depth += [(device(g, 1), device(g, 0)), (device(g, 3), device(g, 2))]
        by_y += [(device(g, 0), device(g - 1, 0)), (device(g, 3), device(g - 1, 3))]
        of_lower += [(device(g, 1), device(g - 1, 2)), (device(g, 2), device(g - 1, 3))]
        of_diag.append((device(g, 2), device(g - 1, 2)))
        for q in range(4):
            up = (device(g, q), device(g, (q + 1) % 4))
            down = (device(g, q), device(g, (q - 1) % 4))
            first_route.append(down if g >= half else up)
            second_route.append(up if g >= half else down)
    got_depth = lax.ppermute(upper_first, AXES, by_depth)
    got_lower = lax.ppermute(lower, AXES, of_lower)
    got_y = lax.ppermute(upper, AXES, by_y)
    got_diag = lax.ppermute(diag, AXES, of_diag)

    own, first1, second1, first_free, second_free, first_due, second_due = call(
        functools.partial(main_kernel, half),
        (share,) + (half_share,) * 6,
        [pltpu.VMEM((2 * WIDE, WIDE), jnp.bfloat16)],
        20,
        6_000_000_000,
        14_000_000,
        density,
        mask,
        prepared,
        ahead,
        got_depth,
        got_y,
        got_lower,
        got_diag,
    )

    got_first = lax.ppermute(first1, AXES, [r for r in first_route if r[0] % 4 != 1])
    got_second = lax.ppermute(second1, AXES, [r for r in second_route if r[0] % 4 != 1])
    first_free = lax.ppermute(first_free, AXES, [r for r in first_route if r[0] % 4 != 1])
    second_free = lax.ppermute(second_free, AXES, [r for r in second_route if r[0] % 4 != 1])
    first_due, second_due = call(
        add_kernel,
        (half_share,) * 2,
        [],
        16,
        1_000_000,
        3_000_000,
        first_due,
        second_due,
        got_first,
        got_second,
    )
    first_due = lax.ppermute(first_due, AXES, first_route)
    second_due = lax.ppermute(second_due, AXES, second_route)
    (out,) = call(
        final_kernel,
        (share,),
        [pltpu.VMEM((ROWS, TILE), jnp.float32)],
        16,
        1_500_000,
        2_700_000,
        own,
        first_free,
        second_free,
        first_due,
        second_due,
        keep_filter,
    )
    return out


def solution(mesh):
    placed = (
        P(("row", "col"), None, "depth"),
        P(("row", "col"), "depth"),
        P(("row", "col"), "depth"),
    )
    groups = mesh.shape["row"] * mesh.shape["col"]
    return jax.shard_map(
        functools.partial(per_device, groups),
        mesh=mesh,
        in_specs=placed,
        out_specs=P(("row", "col"), None, "depth"),
        check_vma=False,
    )
```

```python
import functools
import jax
import jax.numpy as jnp
from jax import lax
from jax.experimental import pallas as pl
from jax.experimental.pallas import tpu as pltpu
from jax.sharding import PartitionSpec as P

BS = 64
ROWS = 16
WIDE = ROWS * BS
HALF = WIDE // 2
TILE = 256
AXES = ("row", "col", "depth")
NT = (((1,), (1,)), ((), ()))
NN = (((1,), (0,)), ((), ()))


def dot(a, b, dims):
    return lax.dot_general(a, b, dims, preferred_element_type=jnp.float32)


def expand(flags, cols):
    count = flags.shape[1]
    slot = lax.broadcasted_iota(jnp.int32, (count, cols), 0)
    col = lax.broadcasted_iota(jnp.int32, (count, cols), 1)
    spread = jnp.where((col >= slot * BS) & (col < slot * BS + BS), 1.0, 0.0)
    return dot(flags.astype(jnp.float32), spread, NN)


def masked_lanes(dens, mask, i, lo, hi):
    m = jnp.broadcast_to(mask[i : i + 1, lo:hi], (16, hi - lo)).astype(jnp.bfloat16)
    x = dens[i, :, lo:hi].reshape(BS // 16, 16, hi - lo)
    return (x * m[None]).reshape(BS, hi - lo)


def late_half(groups_half):
    group = lax.axis_index("row") * lax.axis_size("col") + lax.axis_index("col")
    return group >= groups_half


def upper_width(i):
    return WIDE - 128 * (i // 2)


def lower_width(i):
    return 128 * ((i - 1) // 2 + 1)


def lower_place(i):
    a, e = (i - 1) // 2, (i - 1) % 2
    width = lower_width(i)
    if a < 3:
        return [(2 * (2 * a + e) + 1, HALF - width, 0, width)]
    if a == 3:
        return [(12 + e, 0, 0, width)]
    row = 7 if i == ROWS - 1 else 2 * (6 - a) + e
    return [(2 * row, 0, 0, HALF), (2 * row + 1, 0, HALF, width - HALF)]


def put_upper(own, put):
    put(0, own(0, 0, HALF))
    put(1, own(0, HALF, WIDE))
    for i in range(1, 9):
        put(1 + i, own(i, 0, HALF))
    for i in range(1, 8):
        left = own(i, HALF, WIDE - 128 * (i // 2))[:, : HALF - BS * i]
        right = own(ROWS - i, 0, 128 * ((i + 1) // 2))[:, : BS * i]
        put(9 + i, jnp.concatenate([left, right], axis=1))


def pack(dens, mask, send, lower_at):
    q = lax.axis_index("depth")

    def own(i, lo, hi):
        return masked_lanes(dens, mask, i, lo, hi)

    def put(n, part):
        send[n] = part

    @pl.when(q != lower_at)
    def _():
        put_upper(own, put)

    @pl.when(q == lower_at)
    def _():
        for i in range(1, ROWS):
            width = lower_width(i)
            part = own(i, WIDE - width, WIDE)
            for n, lane, first, lanes in lower_place(i):
                send[n, :, lane : lane + lanes] = part[:, first : first + lanes]
        send[16] = jnp.zeros((BS, HALF), jnp.bfloat16)


def pack_kernel(dens, pat, send, diag, mask):
    mask[...] = expand(pat[...], WIDE)
    pack(dens, mask, send, 1)
    for a in range(ROWS // 2):
        pair = [masked_lanes(dens, mask, 2 * a + e, 0, 2 * BS)[:, :BS] for e in range(2)]
        diag[a] = jnp.concatenate(pair, axis=1)


def pack_first_kernel(dens, mask, send):
    pack(dens, mask, send, 2)


def own_parts(dens, mask):
    def upper(i):
        return masked_lanes(dens, mask, i, 0, upper_width(i))

    def lower(i):
        return masked_lanes(dens, mask, i, WIDE - lower_width(i), WIDE)

    return lower, upper


def sent_upper(buf):
    def get(i):
        if i == 0:
            return jnp.concatenate([buf[0], buf[1]], axis=1)
        if i < 8:
            rest = HALF - 128 * (i // 2)
            return jnp.concatenate([buf[1 + i], buf[9 + i, :, :rest]], axis=1)
        return buf[9 + ROWS - i if i > 8 else 9]

    return get


def sent_lower(buf):
    def get(i):
        pieces = [buf[n, :, lane : lane + lanes] for n, lane, _, lanes in lower_place(i)]
        return pieces[0] if len(pieces) == 1 else jnp.concatenate(pieces, axis=1)

    return get


def build(dst, base, lower, upper, packed=False):
    lane = lax.broadcasted_iota(jnp.int32, (BS, WIDE), 1)
    for i in range(ROWS):
        rows = slice(base + i * BS, base + (i + 1) * BS)
        parts = []
        if i > 0:
            parts.append(lower(i) if lower else jnp.zeros((BS, lower_width(i)), jnp.bfloat16))
        placed = packed and i >= 8
        if upper and not placed:
            parts.append(upper(i))
        else:
            parts.append(jnp.zeros((BS, upper_width(i)), jnp.bfloat16))
        both = jnp.concatenate(parts, axis=1) if i > 0 else parts[0]
        if i % 2:
            both = both[:, BS : BS + WIDE]
            if not lower:
                both = jnp.where(lane >= i * BS, both, jnp.zeros_like(both))
            if not upper or placed:
                both = jnp.where(lane < i * BS, both, jnp.zeros_like(both))
        if placed:
            dst[rows, :HALF] = both[:, :HALF]
            right = jnp.where(lane[:, HALF:] >= i * BS, upper(i), both[:, HALF:])
            dst[rows, HALF:] = right
        else:
            dst[rows, :] = both


def put_diagonal(dst, base, diag):
    lane = lax.broadcasted_iota(jnp.int32, (BS, 2 * BS), 1)
    for i in range(ROWS):
        a = i // 2
        at = (slice(base + i * BS, base + (i + 1) * BS), slice(2 * BS * a, 2 * BS * (a + 1)))
        mine = lane >= BS if i % 2 else lane < BS
        dst[at] = jnp.where(mine, diag[a], dst[at])


def mirror(dst, base, from_lower=False):
    r = lax.broadcasted_iota(jnp.int32, (TILE, TILE), 0)
    c = lax.broadcasted_iota(jnp.int32, (TILE, TILE), 1)
    eye = jnp.where(r == c, 1.0, 0.0).astype(jnp.bfloat16)
    block_r, block_c = lax.shift_right_logical(r, 6), lax.shift_right_logical(c, 6)
    given = block_r > block_c if from_lower else block_r < block_c
    strict = jnp.where(given, 1.0, 0.0).astype(jnp.bfloat16)

    def tile_at(n, m):
        return (slice(base + n * TILE, base + (n + 1) * TILE), slice(m * TILE, (m + 1) * TILE))

    for n in range(WIDE // TILE):
        diag = dst[tile_at(n, n)]
        dst[tile_at(n, n)] = diag + dot(eye, diag * strict, NT).astype(jnp.bfloat16)
        for m in range(n + 1, WIDE // TILE):
            source, target = (tile_at(m, n), tile_at(n, m))
            if not from_lower:
                source, target = target, source
            dst[target] = dot(eye, dst[source], NT).astype(jnp.bfloat16)


def prepare_kernel(dens, mask, y, acc):
    q = lax.axis_index("depth")
    own_lower, own_upper = own_parts(dens, mask)

    @pl.when((q == 0) | (q == 2))
    def _():
        build(y, 0, None, own_upper)

    @pl.when(q == 2)
    def _():
        mirror(y, 0)

    @pl.when(q == 3)
    def _():
        build(y, 0, own_lower, None)

    @pl.when(q != 1)
    def _():
        for t in range(WIDE // TILE):
            lo, hi = t * TILE, (t + 1) * TILE
            acc[t, :, : WIDE - lo] = dot(y[lo:hi, :], y[lo:, :], NT)


def main_kernel(
    groups_half,
    dens,
    mask,
    y,
    acc,
    got_a,
    got_b,
    got_diag,
    own,
    first1,
    second1,
    first_free,
    second_free,
    first_due,
    second_due,
    z,
):
    q = lax.axis_index("depth")
    late = late_half(groups_half)
    own_lower, own_upper = own_parts(dens, mask)

    def finish(static_q, tile_row, window):
        for n in range(TILE // BS):
            i = tile_row * (TILE // BS) + n
            row = window[n * BS : (n + 1) * BS, n * BS : n * BS + WIDE].astype(jnp.bfloat16)

            def share(p):
                p = p % 4
                return row[:, p * TILE : (p + 1) * TILE]

            own[i] = share(static_q)
            first = jnp.where(late, share(static_q - 1), share(static_q + 1))
            second = jnp.where(late, share(static_q + 1), share(static_q - 1))
            if i < 8:
                first1[i] = share(static_q + 2)
                first_due[i] = first
                second_free[i] = second
            else:
                second1[i - 8] = share(static_q + 2)
                first_free[i - 8] = first
                second_due[i - 8] = second

    def products(static_q):
        for t in range(WIDE // TILE):
            lo, hi = t * TILE, (t + 1) * TILE
            ahead = acc[t, :, : WIDE - lo]
            if static_q == 3:
                later = dot(y[lo:hi, :hi], z[WIDE : WIDE + hi, :hi], NT)
                window = jnp.concatenate([ahead, later], axis=1)
            else:
                window = dot(z[lo:hi, :], z[lo : lo + WIDE + TILE, :], NT)
                later = window[:, WIDE - lo :]
                if static_q == 2:
                    later = later + dot(y[lo:hi, :], z[:WIDE, :hi], NN)
                window = jnp.concatenate([window[:, : WIDE - lo] + ahead, later], axis=1)
            finish(static_q, t, window)

    @pl.when(q == 0)
    def _():
        build(z, 0, own_lower, sent_upper(got_a), True)
        build(z, WIDE, None, sent_upper(got_b), True)
        products(0)

    @pl.when(q == 1)
    def _():
        for ref in (own, first_free, second_free, first_due, second_due):
            ref[...] = jnp.zeros_like(ref)

    @pl.when(q == 2)
    def _():
        build(z, 0, own_lower, sent_upper(got_a), True)
        build(z, WIDE, sent_lower(got_b), None)
        put_diagonal(z, WIDE, got_diag)
        mirror(z, WIDE, True)
        products(2)

    @pl.when(q == 3)
    def _():
        build(z, WIDE, sent_lower(got_a), sent_upper(got_b), True)
        products(3)


def add_kernel(first, second, got_first, got_second, first_out, second_out):
    for i in range(8):
        total = first[i].astype(jnp.float32) + got_first[i].astype(jnp.float32)
        first_out[i] = total.astype(jnp.bfloat16)
        total = second[i].astype(jnp.float32) + got_second[i].astype(jnp.float32)
        second_out[i] = total.astype(jnp.bfloat16)


def final_kernel(own, first_free, second_free, first_due, second_due, keep, out, mask):
    mask[...] = expand(keep[...], TILE)
    for i in range(ROWS):
        one, other = (first_due, second_free) if i < 8 else (first_free, second_due)
        total = own[i].astype(jnp.float32) + one[i % 8].astype(jnp.float32)
        total = total + other[i % 8].astype(jnp.float32)
        out[i] = (total * mask[i : i + 1, :]).astype(jnp.bfloat16)


def vmem(count):
    return [pl.BlockSpec(memory_space=pltpu.VMEM)] * count


def per_device(groups, density, pattern, keep_filter):
    mib = 1024 * 1024
    window_rows = (WIDE // TILE, TILE, WIDE)
    slot_mask = (ROWS, WIDE)
    wide_types = (window_rows, slot_mask)

    def call(kernel, outs, scratch, limit, flops, moved, *operands):
        return pl.pallas_call(
            kernel,
            out_shape=tuple(
                jax.ShapeDtypeStruct(shape, jnp.float32 if shape in wide_types else jnp.bfloat16)
                for shape in outs
            ),
            in_specs=vmem(len(operands)),
            out_specs=tuple(vmem(len(outs))),
            scratch_shapes=scratch,
            compiler_params=pltpu.CompilerParams(vmem_limit_bytes=limit * mib),
            cost_estimate=pl.CostEstimate(flops=flops, bytes_accessed=moved, transcendentals=0),
        )(*operands)

    packed = (17, BS, HALF)
    share = (ROWS, BS, TILE)
    half_share = (ROWS // 2, BS, TILE)
    half = groups // 2

    send_b, diag, mask = call(
        pack_kernel,
        (packed, (ROWS // 2, BS, 2 * BS), slot_mask),
        [],
        16,
        4_000_000,
        3_500_000,
        density,
        pattern,
    )
    (send_a,) = call(
        pack_first_kernel,
        (packed,),
        [],
        16,
        4_000_000,
        4_500_000,
        density,
        mask,
    )
    prepared, ahead = call(
        prepare_kernel,
        ((WIDE, WIDE), window_rows),
        [],
        16,
        3_000_000_000,
        9_500_000,
        density,
        mask,
    )

    def device(g, q):
        return (g % groups) * 4 + q

    route_a, route_b, route_diag, first_route, second_route = [], [], [], [], []
    for g in range(groups):
        route_a += [(device(g, 1), device(g, 0)), (device(g, 3), device(g, 2))]
        route_a.append((device(g, 2), device(g - 1, 3)))
        route_b += [(device(g, 0), device(g - 1, 0)), (device(g, 3), device(g - 1, 3))]
        route_b.append((device(g, 1), device(g - 1, 2)))
        route_diag.append((device(g, 2), device(g - 1, 2)))
        for q in range(4):
            up = (device(g, q), device(g, (q + 1) % 4))
            down = (device(g, q), device(g, (q - 1) % 4))
            first_route.append(down if g >= half else up)
            second_route.append(up if g >= half else down)
    got_a = lax.ppermute(send_a, AXES, route_a)
    got_b = lax.ppermute(send_b, AXES, route_b)
    got_diag = lax.ppermute(diag, AXES, route_diag)

    own, first1, second1, first_free, second_free, first_due, second_due = call(
        functools.partial(main_kernel, half),
        (share,) + (half_share,) * 6,
        [pltpu.VMEM((2 * WIDE, WIDE), jnp.bfloat16)],
        20,
        6_000_000_000,
        14_000_000,
        density,
        mask,
        prepared,
        ahead,
        got_a,
        got_b,
        got_diag,
    )

    got_first = lax.ppermute(first1, AXES, [r for r in first_route if r[0] % 4 != 1])
    got_second = lax.ppermute(second1, AXES, [r for r in second_route if r[0] % 4 != 1])
    first_free = lax.ppermute(first_free, AXES, [r for r in first_route if r[0] % 4 != 1])
    second_free = lax.ppermute(second_free, AXES, [r for r in second_route if r[0] % 4 != 1])
    first_due, second_due = call(
        add_kernel,
        (half_share,) * 2,
        [],
        16,
        1_000_000,
        3_000_000,
        first_due,
        second_due,
        got_first,
        got_second,
    )
    first_due = lax.ppermute(first_due, AXES, first_route)
    second_due = lax.ppermute(second_due, AXES, second_route)
    (out,) = call(
        final_kernel,
        (share,),
        [pltpu.VMEM((ROWS, TILE), jnp.float32)],
        16,
        1_500_000,
        2_700_000,
        own,
        first_free,
        second_free,
        first_due,
        second_due,
        keep_filter,
    )
    return out


def solution(mesh):
    placed = (
        P(("row", "col"), None, "depth"),
        P(("row", "col"), "depth"),
        P(("row", "col"), "depth"),
    )
    groups = mesh.shape["row"] * mesh.shape["col"]
    return jax.shard_map(
        functools.partial(per_device, groups),
        mesh=mesh,
        in_specs=placed,
        out_specs=P(("row", "col"), None, "depth"),
        check_vma=False,
    )
```

```python
import functools
import jax
import jax.numpy as jnp
from jax import lax
from jax.experimental import pallas as pl
from jax.experimental.pallas import tpu as pltpu
from jax.sharding import PartitionSpec as P

BS = 64
ROWS = 16
WIDE = ROWS * BS
HALF = WIDE // 2
TILE = 256
AXES = ("row", "col", "depth")
NT = (((1,), (1,)), ((), ()))
NN = (((1,), (0,)), ((), ()))


def dot(a, b, dims):
    return lax.dot_general(a, b, dims, preferred_element_type=jnp.float32)


def expand(flags, cols):
    count = flags.shape[1]
    slot = lax.broadcasted_iota(jnp.int32, (count, cols), 0)
    col = lax.broadcasted_iota(jnp.int32, (count, cols), 1)
    spread = jnp.where((col >= slot * BS) & (col < slot * BS + BS), 1.0, 0.0)
    return dot(flags.astype(jnp.float32), spread, NN)


def masked_lanes(dens, mask, i, lo, hi):
    m = jnp.broadcast_to(mask[i : i + 1, lo:hi], (16, hi - lo)).astype(jnp.bfloat16)
    x = dens[i, :, lo:hi].reshape(BS // 16, 16, hi - lo)
    return (x * m[None]).reshape(BS, hi - lo)


def late_half(groups_half):
    group = lax.axis_index("row") * lax.axis_size("col") + lax.axis_index("col")
    return group >= groups_half


def upper_width(i):
    return WIDE - 128 * (i // 2)


def lower_width(i):
    return 128 * ((i - 1) // 2 + 1)


def put_upper(own, put):
    put(0, own(0, 0, HALF))
    put(1, own(0, HALF, WIDE))
    for i in range(1, 9):
        put(1 + i, own(i, 0, HALF))
    for i in range(1, 8):
        left = own(i, HALF, WIDE - 128 * (i // 2))[:, : HALF - BS * i]
        right = own(ROWS - i, 0, 128 * ((i + 1) // 2))[:, : BS * i]
        put(9 + i, jnp.concatenate([left, right], axis=1))


def put_lower(own, put):
    for i in range(8, ROWS):
        put(i - 8, own(i, HALF, WIDE))
    for r in range(1, 8):
        odd = BS * (r % 2)
        left = own(8 - r, HALF + 128 * (r // 2), WIDE)[:, odd:]
        right = own(8 + r, HALF - 128 * ((r + 1) // 2), HALF)[:, odd:]
        put(7 + r, jnp.concatenate([left, right], axis=1))


def pack_kernel(dens, pat, upper, diag, mask):
    mask[...] = expand(pat[...], WIDE)

    def own(i, lo, hi):
        return masked_lanes(dens, mask, i, lo, hi)

    def put(n, part):
        upper[n] = part

    put_upper(own, put)
    for a in range(ROWS // 2):
        pair = [own(2 * a + e, 0, 2 * BS)[:, :BS] for e in range(2)]
        diag[a] = jnp.concatenate(pair, axis=1)


def pack_first_kernel(dens, mask, lower, upper):
    def own(i, lo, hi):
        return masked_lanes(dens, mask, i, lo, hi)

    def put_low(n, part):
        lower[n] = part

    def put_up(n, part):
        upper[n] = part

    put_lower(own, put_low)
    put_upper(own, put_up)


def own_parts(dens, mask):
    def upper(i):
        return masked_lanes(dens, mask, i, 0, upper_width(i))

    def lower(i):
        return masked_lanes(dens, mask, i, WIDE - lower_width(i), WIDE)

    return lower, upper


def sent_upper(buf):
    def get(i):
        if i == 0:
            return jnp.concatenate([buf[0], buf[1]], axis=1)
        if i < 8:
            rest = HALF - 128 * (i // 2)
            return jnp.concatenate([buf[1 + i], buf[9 + i, :, :rest]], axis=1)
        return buf[9 + ROWS - i if i > 8 else 9]

    return get


def sent_lower(buf):
    def get(i):
        if i < 8:
            return buf[15 - i]
        if i == 8:
            return buf[0]
        return jnp.concatenate([buf[i - 1, :, HALF - 128 * ((i - 7) // 2) :], buf[i - 8]], axis=1)

    return get


def build(dst, base, lower, upper, packed_lower=False, packed_upper=False):
    lane = lax.broadcasted_iota(jnp.int32, (BS, WIDE), 1)
    for i in range(ROWS):
        rows = slice(base + i * BS, base + (i + 1) * BS)
        low_placed = packed_lower and 0 < i < 8
        up_placed = packed_upper and i >= 8
        shifted_lower = lower and not low_placed
        shifted_upper = upper and not up_placed
        parts = []
        if i > 0:
            zeros = jnp.zeros((BS, lower_width(i)), jnp.bfloat16)
            parts.append(lower(i) if shifted_lower else zeros)
        zeros = jnp.zeros((BS, upper_width(i)), jnp.bfloat16)
        parts.append(upper(i) if shifted_upper else zeros)
        both = jnp.concatenate(parts, axis=1) if i > 0 else parts[0]
        if i % 2:
            both = both[:, BS : BS + WIDE]
            if not shifted_lower:
                both = jnp.where(lane >= i * BS, both, jnp.zeros_like(both))
            if not shifted_upper:
                both = jnp.where(lane < i * BS, both, jnp.zeros_like(both))
        left, right = both[:, :HALF], both[:, HALF:]
        if low_placed:
            left = jnp.where(lane[:, :HALF] < i * BS, lower(i), left)
        if up_placed:
            right = jnp.where(lane[:, HALF:] >= i * BS, upper(i), right)
        dst[rows, :HALF] = left
        dst[rows, HALF:] = right


def put_diagonal(dst, base, diag):
    lane = lax.broadcasted_iota(jnp.int32, (BS, 2 * BS), 1)
    for i in range(ROWS):
        a = i // 2
        at = (slice(base + i * BS, base + (i + 1) * BS), slice(2 * BS * a, 2 * BS * (a + 1)))
        mine = lane >= BS if i % 2 else lane < BS
        dst[at] = jnp.where(mine, diag[a], dst[at])


def mirror(dst, base, from_lower=False):
    r = lax.broadcasted_iota(jnp.int32, (TILE, TILE), 0)
    c = lax.broadcasted_iota(jnp.int32, (TILE, TILE), 1)
    eye = jnp.where(r == c, 1.0, 0.0).astype(jnp.bfloat16)
    block_r, block_c = lax.shift_right_logical(r, 6), lax.shift_right_logical(c, 6)
    given = block_r > block_c if from_lower else block_r < block_c
    strict = jnp.where(given, 1.0, 0.0).astype(jnp.bfloat16)

    def tile_at(n, m):
        return (slice(base + n * TILE, base + (n + 1) * TILE), slice(m * TILE, (m + 1) * TILE))

    for n in range(WIDE // TILE):
        diag = dst[tile_at(n, n)]
        dst[tile_at(n, n)] = diag + dot(eye, diag * strict, NT).astype(jnp.bfloat16)
        for m in range(n + 1, WIDE // TILE):
            source, target = (tile_at(m, n), tile_at(n, m))
            if not from_lower:
                source, target = target, source
            dst[target] = dot(eye, dst[source], NT).astype(jnp.bfloat16)


def prepare_kernel(dens, mask, y, acc):
    q = lax.axis_index("depth")
    own_lower, own_upper = own_parts(dens, mask)

    @pl.when((q == 0) | (q == 2))
    def _():
        build(y, 0, None, own_upper)

    @pl.when(q == 2)
    def _():
        mirror(y, 0)

    @pl.when(q == 3)
    def _():
        build(y, 0, own_lower, None)

    @pl.when(q != 1)
    def _():
        for t in range(WIDE // TILE):
            lo, hi = t * TILE, (t + 1) * TILE
            acc[t, :, : WIDE - lo] = dot(y[lo:hi, :], y[lo:, :], NT)


def main_kernel(
    groups_half,
    dens,
    mask,
    y,
    acc,
    got_lower,
    got_depth,
    got_y,
    got_diag,
    own,
    first1,
    second1,
    first_free,
    second_free,
    first_due,
    second_due,
    z,
):
    q = lax.axis_index("depth")
    late = late_half(groups_half)
    own_lower, own_upper = own_parts(dens, mask)

    def finish(static_q, tile_row, window):
        for n in range(TILE // BS):
            i = tile_row * (TILE // BS) + n
            row = window[n * BS : (n + 1) * BS, n * BS : n * BS + WIDE].astype(jnp.bfloat16)

            def share(p):
                p = p % 4
                return row[:, p * TILE : (p + 1) * TILE]

            own[i] = share(static_q)
            first = jnp.where(late, share(static_q - 1), share(static_q + 1))
            second = jnp.where(late, share(static_q + 1), share(static_q - 1))
            if i < 8:
                first1[i] = share(static_q + 2)
                first_due[i] = first
                second_free[i] = second
            else:
                second1[i - 8] = share(static_q + 2)
                first_free[i - 8] = first
                second_due[i - 8] = second

    def products(static_q):
        for t in range(WIDE // TILE):
            lo, hi = t * TILE, (t + 1) * TILE
            ahead = acc[t, :, : WIDE - lo]
            if static_q == 3:
                later = dot(y[lo:hi, :hi], z[WIDE : WIDE + hi, :hi], NT)
                window = jnp.concatenate([ahead, later], axis=1)
            else:
                window = dot(z[lo:hi, :], z[lo : lo + WIDE + TILE, :], NT)
                later = window[:, WIDE - lo :]
                if static_q == 2:
                    later = later + dot(y[lo:hi, :], z[:WIDE, :hi], NN)
                window = jnp.concatenate([window[:, : WIDE - lo] + ahead, later], axis=1)
            finish(static_q, t, window)

    @pl.when(q == 0)
    def _():
        build(z, 0, own_lower, sent_upper(got_depth), packed_upper=True)
        build(z, WIDE, None, sent_upper(got_y), packed_upper=True)
        products(0)

    @pl.when(q == 1)
    def _():
        for ref in (own, first_free, second_free, first_due, second_due):
            ref[...] = jnp.zeros_like(ref)

    @pl.when(q == 2)
    def _():
        build(z, 0, own_lower, sent_upper(got_depth), packed_upper=True)
        build(z, WIDE, sent_lower(got_lower), None, packed_lower=True)
        put_diagonal(z, WIDE, got_diag)
        mirror(z, WIDE, True)
        products(2)

    @pl.when(q == 3)
    def _():
        build(z, WIDE, sent_lower(got_lower), sent_upper(got_y), True, True)
        products(3)


def add_kernel(first, second, got_first, got_second, first_out, second_out):
    for i in range(8):
        total = first[i].astype(jnp.float32) + got_first[i].astype(jnp.float32)
        first_out[i] = total.astype(jnp.bfloat16)
        total = second[i].astype(jnp.float32) + got_second[i].astype(jnp.float32)
        second_out[i] = total.astype(jnp.bfloat16)


def final_kernel(own, first_free, second_free, first_due, second_due, keep, out, mask):
    mask[...] = expand(keep[...], TILE)
    for i in range(ROWS):
        one, other = (first_due, second_free) if i < 8 else (first_free, second_due)
        total = own[i].astype(jnp.float32) + one[i % 8].astype(jnp.float32)
        total = total + other[i % 8].astype(jnp.float32)
        out[i] = (total * mask[i : i + 1, :]).astype(jnp.bfloat16)


def vmem(count):
    return [pl.BlockSpec(memory_space=pltpu.VMEM)] * count


def per_device(groups, density, pattern, keep_filter):
    mib = 1024 * 1024
    window_rows = (WIDE // TILE, TILE, WIDE)
    slot_mask = (ROWS, WIDE)
    wide_types = (window_rows, slot_mask)

    def call(kernel, outs, scratch, limit, flops, moved, *operands):
        return pl.pallas_call(
            kernel,
            out_shape=tuple(
                jax.ShapeDtypeStruct(shape, jnp.float32 if shape in wide_types else jnp.bfloat16)
                for shape in outs
            ),
            in_specs=vmem(len(operands)),
            out_specs=tuple(vmem(len(outs))),
            scratch_shapes=scratch,
            compiler_params=pltpu.CompilerParams(vmem_limit_bytes=limit * mib),
            cost_estimate=pl.CostEstimate(flops=flops, bytes_accessed=moved, transcendentals=0),
        )(*operands)

    upper_part = (17, BS, HALF)
    lower_part = (15, BS, HALF)
    share = (ROWS, BS, TILE)
    half_share = (ROWS // 2, BS, TILE)
    half = groups // 2

    upper, diag, mask = call(
        pack_kernel,
        (upper_part, (ROWS // 2, BS, 2 * BS), slot_mask),
        [],
        16,
        4_000_000,
        3_500_000,
        density,
        pattern,
    )
    lower, upper_first = call(
        pack_first_kernel,
        (lower_part, upper_part),
        [],
        16,
        4_000_000,
        4_500_000,
        density,
        mask,
    )
    prepared, ahead = call(
        prepare_kernel,
        ((WIDE, WIDE), window_rows),
        [],
        16,
        3_000_000_000,
        9_500_000,
        density,
        mask,
    )

    def device(g, q):
        return (g % groups) * 4 + q

    of_lower, by_depth, by_y, of_diag, first_route, second_route = [], [], [], [], [], []
    for g in range(groups):
        of_lower += [(device(g, 1), device(g - 1, 2)), (device(g, 2), device(g - 1, 3))]
        by_depth += [(device(g, 1), device(g, 0)), (device(g, 3), device(g, 2))]
        by_y += [(device(g, 0), device(g - 1, 0)), (device(g, 3), device(g - 1, 3))]
        of_diag.append((device(g, 2), device(g - 1, 2)))
        for q in range(4):
            up = (device(g, q), device(g, (q + 1) % 4))
            down = (device(g, q), device(g, (q - 1) % 4))
            first_route.append(down if g >= half else up)
            second_route.append(up if g >= half else down)
    got_lower = lax.ppermute(lower, AXES, of_lower)
    got_depth = lax.ppermute(upper_first, AXES, by_depth)
    got_y = lax.ppermute(upper, AXES, by_y)
    got_diag = lax.ppermute(diag, AXES, of_diag)

    own, first1, second1, first_free, second_free, first_due, second_due = call(
        functools.partial(main_kernel, half),
        (share,) + (half_share,) * 6,
        [pltpu.VMEM((2 * WIDE, WIDE), jnp.bfloat16)],
        20,
        6_000_000_000,
        14_000_000,
        density,
        mask,
        prepared,
        ahead,
        got_lower,
        got_depth,
        got_y,
        got_diag,
    )

    got_first = lax.ppermute(first1, AXES, [r for r in first_route if r[0] % 4 != 1])
    got_second = lax.ppermute(second1, AXES, [r for r in second_route if r[0] % 4 != 1])
    first_free = lax.ppermute(first_free, AXES, [r for r in first_route if r[0] % 4 != 1])
    second_free = lax.ppermute(second_free, AXES, [r for r in second_route if r[0] % 4 != 1])
    first_due, second_due = call(
        add_kernel,
        (half_share,) * 2,
        [],
        16,
        1_000_000,
        3_000_000,
        first_due,
        second_due,
        got_first,
        got_second,
    )
    first_due = lax.ppermute(first_due, AXES, first_route)
    second_due = lax.ppermute(second_due, AXES, second_route)
    (out,) = call(
        final_kernel,
        (share,),
        [pltpu.VMEM((ROWS, TILE), jnp.float32)],
        16,
        1_500_000,
        2_700_000,
        own,
        first_free,
        second_free,
        first_due,
        second_due,
        keep_filter,
    )
    return out


def solution(mesh):
    placed = (
        P(("row", "col"), None, "depth"),
        P(("row", "col"), "depth"),
        P(("row", "col"), "depth"),
    )
    groups = mesh.shape["row"] * mesh.shape["col"]
    return jax.shard_map(
        functools.partial(per_device, groups),
        mesh=mesh,
        in_specs=placed,
        out_specs=P(("row", "col"), None, "depth"),
        check_vma=False,
    )
```

```python
import functools
import jax
import jax.numpy as jnp
from jax import lax
from jax.experimental import pallas as pl
from jax.experimental.pallas import tpu as pltpu
from jax.sharding import PartitionSpec as P

BS = 64
ROWS = 16
WIDE = ROWS * BS
HALF = WIDE // 2
TILE = 256
MAIN = 14
AXES = ("row", "col", "depth")
NT = (((1,), (1,)), ((), ()))
NN = (((1,), (0,)), ((), ()))


def dot(a, b, dims):
    return lax.dot_general(a, b, dims, preferred_element_type=jnp.float32)


def expand(flags, cols):
    count = flags.shape[1]
    slot = lax.broadcasted_iota(jnp.int32, (count, cols), 0)
    col = lax.broadcasted_iota(jnp.int32, (count, cols), 1)
    spread = jnp.where((col >= slot * BS) & (col < slot * BS + BS), 1.0, 0.0)
    return dot(flags.astype(jnp.float32), spread, NN)


def masked_lanes(dens, mask, i, lo, hi):
    m = jnp.broadcast_to(mask[i : i + 1, lo:hi], (16, hi - lo)).astype(jnp.bfloat16)
    x = dens[i, :, lo:hi].reshape(BS // 16, 16, hi - lo)
    return (x * m[None]).reshape(BS, hi - lo)


def late_half(groups_half):
    group = lax.axis_index("row") * lax.axis_size("col") + lax.axis_index("col")
    return group >= groups_half


def upper_width(i):
    return WIDE - 128 * (i // 2)


def lower_width(i):
    return 128 * ((i - 1) // 2 + 1)


def put_upper(own, put):
    put(0, own(0, 0, HALF))
    put(1, own(0, HALF, WIDE))
    for i in range(1, 9):
        put(1 + i, own(i, 0, HALF))
    for i in range(1, 8):
        left = own(i, HALF, WIDE - 128 * (i // 2))[:, : HALF - BS * i]
        right = own(ROWS - i, 0, 128 * ((i + 1) // 2))[:, : BS * i]
        put(9 + i, jnp.concatenate([left, right], axis=1))


def put_lower(own, put):
    for i in range(8, ROWS):
        put(i - 8, own(i, HALF, WIDE))
    for r in range(1, 8):
        odd = BS * (r % 2)
        left = own(8 - r, HALF + 128 * (r // 2), WIDE)[:, odd:]
        right = own(8 + r, HALF - 128 * ((r + 1) // 2), HALF)[:, odd:]
        put(7 + r, jnp.concatenate([left, right], axis=1))


def pack_kernel(dens, pat, upper, rest, mask):
    mask[...] = expand(pat[...], WIDE)
    diagonal = lax.axis_index("depth") == 2

    def own(i, lo, hi):
        return masked_lanes(dens, mask, i, lo, hi)

    def put(n, part):
        if n < MAIN:
            upper[n] = part
        else:

            @pl.when(jnp.logical_not(diagonal))
            def _():
                rest[n - MAIN] = part

    put_upper(own, put)

    @pl.when(diagonal)
    def _():
        for a in range(ROWS // 2):
            pair = [own(2 * a + e, 0, 2 * BS)[:, :BS] for e in range(2)]
            lane = 2 * BS * (a % 4)
            rest[a // 4, :, lane : lane + 2 * BS] = jnp.concatenate(pair, axis=1)
        rest[2] = jnp.zeros((BS, HALF), jnp.bfloat16)


def pack_first_kernel(dens, mask, lower, upper):
    def own(i, lo, hi):
        return masked_lanes(dens, mask, i, lo, hi)

    def put_low(n, part):
        lower[n] = part

    def put_up(n, part):
        upper[n] = part

    put_lower(own, put_low)
    put_upper(own, put_up)


def own_parts(dens, mask):
    def upper(i):
        return masked_lanes(dens, mask, i, 0, upper_width(i))

    def lower(i):
        return masked_lanes(dens, mask, i, WIDE - lower_width(i), WIDE)

    return lower, upper


def sent_upper(main, rest=None):
    def part(n, lanes):
        if rest is None or n < MAIN:
            return main[n, :, :lanes]
        return rest[n - MAIN, :, :lanes]

    def get(i):
        if i == 0:
            return jnp.concatenate([part(0, HALF), part(1, HALF)], axis=1)
        if i < 8:
            return jnp.concatenate([part(1 + i, HALF), part(9 + i, HALF - 128 * (i // 2))], axis=1)
        return part(9 + ROWS - i if i > 8 else 9, HALF)

    return get


def sent_lower(buf):
    def get(i):
        if i < 8:
            return buf[15 - i]
        if i == 8:
            return buf[0]
        return jnp.concatenate([buf[i - 1, :, HALF - 128 * ((i - 7) // 2) :], buf[i - 8]], axis=1)

    return get


def build(dst, base, lower, upper, packed_lower=False, packed_upper=False):
    lane = lax.broadcasted_iota(jnp.int32, (BS, WIDE), 1)
    for i in range(ROWS):
        rows = slice(base + i * BS, base + (i + 1) * BS)
        low_placed = packed_lower and 0 < i < 8
        up_placed = packed_upper and i >= 8
        shifted_lower = lower and not low_placed
        shifted_upper = upper and not up_placed
        parts = []
        if i > 0:
            zeros = jnp.zeros((BS, lower_width(i)), jnp.bfloat16)
            parts.append(lower(i) if shifted_lower else zeros)
        zeros = jnp.zeros((BS, upper_width(i)), jnp.bfloat16)
        parts.append(upper(i) if shifted_upper else zeros)
        both = jnp.concatenate(parts, axis=1) if i > 0 else parts[0]
        if i % 2:
            both = both[:, BS : BS + WIDE]
            if not shifted_lower:
                both = jnp.where(lane >= i * BS, both, jnp.zeros_like(both))
            if not shifted_upper:
                both = jnp.where(lane < i * BS, both, jnp.zeros_like(both))
        left, right = both[:, :HALF], both[:, HALF:]
        if low_placed:
            left = jnp.where(lane[:, :HALF] < i * BS, lower(i), left)
        if up_placed:
            right = jnp.where(lane[:, HALF:] >= i * BS, upper(i), right)
        dst[rows, :HALF] = left
        dst[rows, HALF:] = right


def put_diagonal(dst, base, rest):
    lane = lax.broadcasted_iota(jnp.int32, (BS, 2 * BS), 1)
    for i in range(ROWS):
        a = i // 2
        at = (slice(base + i * BS, base + (i + 1) * BS), slice(2 * BS * a, 2 * BS * (a + 1)))
        first = 2 * BS * (a % 4)
        diag = rest[a // 4, :, first : first + 2 * BS]
        mine = lane >= BS if i % 2 else lane < BS
        dst[at] = jnp.where(mine, diag, dst[at])


def mirror(dst, base, from_lower=False):
    r = lax.broadcasted_iota(jnp.int32, (TILE, TILE), 0)
    c = lax.broadcasted_iota(jnp.int32, (TILE, TILE), 1)
    eye = jnp.where(r == c, 1.0, 0.0).astype(jnp.bfloat16)
    block_r, block_c = lax.shift_right_logical(r, 6), lax.shift_right_logical(c, 6)
    given = block_r > block_c if from_lower else block_r < block_c
    strict = jnp.where(given, 1.0, 0.0).astype(jnp.bfloat16)

    def tile_at(n, m):
        return (slice(base + n * TILE, base + (n + 1) * TILE), slice(m * TILE, (m + 1) * TILE))

    for n in range(WIDE // TILE):
        diag = dst[tile_at(n, n)]
        dst[tile_at(n, n)] = diag + dot(eye, diag * strict, NT).astype(jnp.bfloat16)
        for m in range(n + 1, WIDE // TILE):
            source, target = (tile_at(m, n), tile_at(n, m))
            if not from_lower:
                source, target = target, source
            dst[target] = dot(eye, dst[source], NT).astype(jnp.bfloat16)


def prepare_kernel(dens, mask, y, acc):
    q = lax.axis_index("depth")
    own_lower, own_upper = own_parts(dens, mask)

    @pl.when((q == 0) | (q == 2))
    def _():
        build(y, 0, None, own_upper)

    @pl.when(q == 2)
    def _():
        mirror(y, 0)

    @pl.when(q == 3)
    def _():
        build(y, 0, own_lower, None)

    @pl.when(q != 1)
    def _():
        for t in range(WIDE // TILE):
            lo, hi = t * TILE, (t + 1) * TILE
            acc[t, :, : WIDE - lo] = dot(y[lo:hi, :], y[lo:, :], NT)


def main_kernel(
    groups_half,
    dens,
    mask,
    y,
    acc,
    got_lower,
    got_depth,
    got_y,
    got_rest,
    own,
    first1,
    second1,
    first_free,
    second_free,
    first_due,
    second_due,
    z,
):
    q = lax.axis_index("depth")
    late = late_half(groups_half)
    own_lower, own_upper = own_parts(dens, mask)

    def finish(static_q, tile_row, window):
        for n in range(TILE // BS):
            i = tile_row * (TILE // BS) + n
            row = window[n * BS : (n + 1) * BS, n * BS : n * BS + WIDE].astype(jnp.bfloat16)

            def share(p):
                p = p % 4
                return row[:, p * TILE : (p + 1) * TILE]

            own[i] = share(static_q)
            first = jnp.where(late, share(static_q - 1), share(static_q + 1))
            second = jnp.where(late, share(static_q + 1), share(static_q - 1))
            if i < 8:
                first1[i] = share(static_q + 2)
                first_due[i] = first
                second_free[i] = second
            else:
                second1[i - 8] = share(static_q + 2)
                first_free[i - 8] = first
                second_due[i - 8] = second

    def products(static_q):
        for t in range(WIDE // TILE):
            lo, hi = t * TILE, (t + 1) * TILE
            ahead = acc[t, :, : WIDE - lo]
            if static_q == 3:
                later = dot(y[lo:hi, :hi], z[WIDE : WIDE + hi, :hi], NT)
                window = jnp.concatenate([ahead, later], axis=1)
            else:
                window = dot(z[lo:hi, :], z[lo : lo + WIDE + TILE, :], NT)
                later = window[:, WIDE - lo :]
                if static_q == 2:
                    later = later + dot(y[lo:hi, :], z[:WIDE, :hi], NN)
                window = jnp.concatenate([window[:, : WIDE - lo] + ahead, later], axis=1)
            finish(static_q, t, window)

    @pl.when(q == 0)
    def _():
        build(z, 0, own_lower, sent_upper(got_depth), packed_upper=True)
        build(z, WIDE, None, sent_upper(got_y, got_rest), packed_upper=True)
        products(0)

    @pl.when(q == 1)
    def _():
        for ref in (own, first_free, second_free, first_due, second_due):
            ref[...] = jnp.zeros_like(ref)

    @pl.when(q == 2)
    def _():
        build(z, 0, own_lower, sent_upper(got_depth), packed_upper=True)
        build(z, WIDE, sent_lower(got_lower), None, packed_lower=True)
        put_diagonal(z, WIDE, got_rest)
        mirror(z, WIDE, True)
        products(2)

    @pl.when(q == 3)
    def _():
        build(z, WIDE, sent_lower(got_lower), sent_upper(got_y, got_rest), True, True)
        products(3)


def add_kernel(first, second, got_first, got_second, first_out, second_out):
    for i in range(8):
        total = first[i].astype(jnp.float32) + got_first[i].astype(jnp.float32)
        first_out[i] = total.astype(jnp.bfloat16)
        total = second[i].astype(jnp.float32) + got_second[i].astype(jnp.float32)
        second_out[i] = total.astype(jnp.bfloat16)


def final_kernel(own, first_free, second_free, first_due, second_due, keep, out, mask):
    mask[...] = expand(keep[...], TILE)
    for i in range(ROWS):
        one, other = (first_due, second_free) if i < 8 else (first_free, second_due)
        total = own[i].astype(jnp.float32) + one[i % 8].astype(jnp.float32)
        total = total + other[i % 8].astype(jnp.float32)
        out[i] = (total * mask[i : i + 1, :]).astype(jnp.bfloat16)


def vmem(count):
    return [pl.BlockSpec(memory_space=pltpu.VMEM)] * count


def per_device(groups, density, pattern, keep_filter):
    mib = 1024 * 1024
    window_rows = (WIDE // TILE, TILE, WIDE)
    slot_mask = (ROWS, WIDE)
    wide_types = (window_rows, slot_mask)

    def call(kernel, outs, scratch, limit, flops, moved, *operands):
        return pl.pallas_call(
            kernel,
            out_shape=tuple(
                jax.ShapeDtypeStruct(shape, jnp.float32 if shape in wide_types else jnp.bfloat16)
                for shape in outs
            ),
            in_specs=vmem(len(operands)),
            out_specs=tuple(vmem(len(outs))),
            scratch_shapes=scratch,
            compiler_params=pltpu.CompilerParams(vmem_limit_bytes=limit * mib),
            cost_estimate=pl.CostEstimate(flops=flops, bytes_accessed=moved, transcendentals=0),
        )(*operands)

    upper_part = (17, BS, HALF)
    lower_part = (15, BS, HALF)
    share = (ROWS, BS, TILE)
    half_share = (ROWS // 2, BS, TILE)
    half = groups // 2

    upper, rest, mask = call(
        pack_kernel,
        ((MAIN, BS, HALF), (17 - MAIN, BS, HALF), slot_mask),
        [],
        16,
        4_000_000,
        3_500_000,
        density,
        pattern,
    )
    lower, upper_first = call(
        pack_first_kernel,
        (lower_part, upper_part),
        [],
        16,
        4_000_000,
        4_500_000,
        density,
        mask,
    )
    prepared, ahead = call(
        prepare_kernel,
        ((WIDE, WIDE), window_rows),
        [],
        16,
        3_000_000_000,
        9_500_000,
        density,
        mask,
    )

    def device(g, q):
        return (g % groups) * 4 + q

    of_lower, by_depth, by_y, of_rest, first_route, second_route = [], [], [], [], [], []
    for g in range(groups):
        of_lower += [(device(g, 1), device(g - 1, 2)), (device(g, 2), device(g - 1, 3))]
        by_depth += [(device(g, 1), device(g, 0)), (device(g, 3), device(g, 2))]
        by_y += [(device(g, 0), device(g - 1, 0)), (device(g, 3), device(g - 1, 3))]
        of_rest += by_y[-2:] + [(device(g, 2), device(g - 1, 2))]
        for q in range(4):
            up = (device(g, q), device(g, (q + 1) % 4))
            down = (device(g, q), device(g, (q - 1) % 4))
            first_route.append(down if g >= half else up)
            second_route.append(up if g >= half else down)
    got_lower = lax.ppermute(lower, AXES, of_lower)
    got_depth = lax.ppermute(upper_first, AXES, by_depth)
    got_y = lax.ppermute(upper, AXES, by_y)
    got_rest = lax.ppermute(rest, AXES, of_rest)

    own, first1, second1, first_free, second_free, first_due, second_due = call(
        functools.partial(main_kernel, half),
        (share,) + (half_share,) * 6,
        [pltpu.VMEM((2 * WIDE, WIDE), jnp.bfloat16)],
        20,
        6_000_000_000,
        14_000_000,
        density,
        mask,
        prepared,
        ahead,
        got_lower,
        got_depth,
        got_y,
        got_rest,
    )

    got_first = lax.ppermute(first1, AXES, [r for r in first_route if r[0] % 4 != 1])
    got_second = lax.ppermute(second1, AXES, [r for r in second_route if r[0] % 4 != 1])
    first_free = lax.ppermute(first_free, AXES, [r for r in first_route if r[0] % 4 != 1])
    second_free = lax.ppermute(second_free, AXES, [r for r in second_route if r[0] % 4 != 1])
    first_due, second_due = call(
        add_kernel,
        (half_share,) * 2,
        [],
        16,
        1_000_000,
        3_000_000,
        first_due,
        second_due,
        got_first,
        got_second,
    )
    first_due = lax.ppermute(first_due, AXES, first_route)
    second_due = lax.ppermute(second_due, AXES, second_route)
    (out,) = call(
        final_kernel,
        (share,),
        [pltpu.VMEM((ROWS, TILE), jnp.float32)],
        16,
        1_500_000,
        2_700_000,
        own,
        first_free,
        second_free,
        first_due,
        second_due,
        keep_filter,
    )
    return out


def solution(mesh):
    placed = (
        P(("row", "col"), None, "depth"),
        P(("row", "col"), "depth"),
        P(("row", "col"), "depth"),
    )
    groups = mesh.shape["row"] * mesh.shape["col"]
    return jax.shard_map(
        functools.partial(per_device, groups),
        mesh=mesh,
        in_specs=placed,
        out_specs=P(("row", "col"), None, "depth"),
        check_vma=False,
    )
```

```python
import functools
import jax
import jax.numpy as jnp
from jax import lax
from jax.experimental import pallas as pl
from jax.experimental.pallas import tpu as pltpu
from jax.sharding import PartitionSpec as P

BS = 64
ROWS = 16
WIDE = ROWS * BS
HALF = WIDE // 2
TILE = 256
MAIN = 15
AXES = ("row", "col", "depth")
NT = (((1,), (1,)), ((), ()))
NN = (((1,), (0,)), ((), ()))


def dot(a, b, dims):
    return lax.dot_general(a, b, dims, preferred_element_type=jnp.float32)


def expand(flags, cols):
    count = flags.shape[1]
    slot = lax.broadcasted_iota(jnp.int32, (count, cols), 0)
    col = lax.broadcasted_iota(jnp.int32, (count, cols), 1)
    spread = jnp.where((col >= slot * BS) & (col < slot * BS + BS), 1.0, 0.0)
    return dot(flags.astype(jnp.float32), spread, NN)


def masked_lanes(dens, mask, i, lo, hi):
    m = jnp.broadcast_to(mask[i : i + 1, lo:hi], (16, hi - lo)).astype(jnp.bfloat16)
    x = dens[i, :, lo:hi].reshape(BS // 16, 16, hi - lo)
    return (x * m[None]).reshape(BS, hi - lo)


def late_half(groups_half):
    group = lax.axis_index("row") * lax.axis_size("col") + lax.axis_index("col")
    return group >= groups_half


def upper_width(i):
    return WIDE - 128 * (i // 2)


def lower_width(i):
    return 128 * ((i - 1) // 2 + 1)


def put_upper(own, put):
    put(0, own(0, 0, HALF))
    put(1, own(0, HALF, WIDE))
    for i in range(1, 9):
        put(1 + i, own(i, 0, HALF))
    for i in range(1, 8):
        left = own(i, HALF, WIDE - 128 * (i // 2))[:, : HALF - BS * i]
        right = own(ROWS - i, 0, 128 * ((i + 1) // 2))[:, : BS * i]
        put(9 + i, jnp.concatenate([left, right], axis=1))


def put_lower(own, put):
    for i in range(8, ROWS):
        put(i - 8, own(i, HALF, WIDE))
    for r in range(1, 8):
        odd = BS * (r % 2)
        left = own(8 - r, HALF + 128 * (r // 2), WIDE)[:, odd:]
        right = own(8 + r, HALF - 128 * ((r + 1) // 2), HALF)[:, odd:]
        put(7 + r, jnp.concatenate([left, right], axis=1))


def pack_kernel(dens, pat, upper, rest, mask):
    mask[...] = expand(pat[...], WIDE)
    diagonal = lax.axis_index("depth") == 2

    def own(i, lo, hi):
        return masked_lanes(dens, mask, i, lo, hi)

    def put(n, part):
        if n < MAIN:
            upper[n] = part
        else:

            @pl.when(jnp.logical_not(diagonal))
            def _():
                rest[n - MAIN] = part

    put_upper(own, put)

    @pl.when(diagonal)
    def _():
        for a in range(ROWS // 2):
            pair = [own(2 * a + e, 0, 2 * BS)[:, :BS] for e in range(2)]
            lane = 2 * BS * (a % 4)
            rest[a // 4, :, lane : lane + 2 * BS] = jnp.concatenate(pair, axis=1)


def pack_first_kernel(dens, mask, lower, upper):
    def own(i, lo, hi):
        return masked_lanes(dens, mask, i, lo, hi)

    def put_low(n, part):
        lower[n] = part

    def put_up(n, part):
        upper[n] = part

    put_lower(own, put_low)
    put_upper(own, put_up)


def own_parts(dens, mask):
    def upper(i):
        return masked_lanes(dens, mask, i, 0, upper_width(i))

    def lower(i):
        return masked_lanes(dens, mask, i, WIDE - lower_width(i), WIDE)

    return lower, upper


def sent_upper(main, rest=None):
    def part(n, lanes):
        if rest is None or n < MAIN:
            return main[n, :, :lanes]
        return rest[n - MAIN, :, :lanes]

    def get(i):
        if i == 0:
            return jnp.concatenate([part(0, HALF), part(1, HALF)], axis=1)
        if i < 8:
            return jnp.concatenate([part(1 + i, HALF), part(9 + i, HALF - 128 * (i // 2))], axis=1)
        return part(9 + ROWS - i if i > 8 else 9, HALF)

    return get


def sent_lower(buf):
    def get(i):
        if i < 8:
            return buf[15 - i]
        if i == 8:
            return buf[0]
        return jnp.concatenate([buf[i - 1, :, HALF - 128 * ((i - 7) // 2) :], buf[i - 8]], axis=1)

    return get


def build(dst, base, lower, upper, packed_lower=False, packed_upper=False):
    lane = lax.broadcasted_iota(jnp.int32, (BS, WIDE), 1)
    for i in range(ROWS):
        rows = slice(base + i * BS, base + (i + 1) * BS)
        low_placed = packed_lower and 0 < i < 8
        up_placed = packed_upper and i >= 8
        shifted_lower = lower and not low_placed
        shifted_upper = upper and not up_placed
        parts = []
        if i > 0:
            zeros = jnp.zeros((BS, lower_width(i)), jnp.bfloat16)
            parts.append(lower(i) if shifted_lower else zeros)
        zeros = jnp.zeros((BS, upper_width(i)), jnp.bfloat16)
        parts.append(upper(i) if shifted_upper else zeros)
        both = jnp.concatenate(parts, axis=1) if i > 0 else parts[0]
        if i % 2:
            both = both[:, BS : BS + WIDE]
            if not shifted_lower:
                both = jnp.where(lane >= i * BS, both, jnp.zeros_like(both))
            if not shifted_upper:
                both = jnp.where(lane < i * BS, both, jnp.zeros_like(both))
        left, right = both[:, :HALF], both[:, HALF:]
        if low_placed:
            left = jnp.where(lane[:, :HALF] < i * BS, lower(i), left)
        if up_placed:
            right = jnp.where(lane[:, HALF:] >= i * BS, upper(i), right)
        dst[rows, :HALF] = left
        dst[rows, HALF:] = right


def put_diagonal(dst, base, rest):
    lane = lax.broadcasted_iota(jnp.int32, (BS, 2 * BS), 1)
    for i in range(ROWS):
        a = i // 2
        at = (slice(base + i * BS, base + (i + 1) * BS), slice(2 * BS * a, 2 * BS * (a + 1)))
        first = 2 * BS * (a % 4)
        diag = rest[a // 4, :, first : first + 2 * BS]
        mine = lane >= BS if i % 2 else lane < BS
        dst[at] = jnp.where(mine, diag, dst[at])


def mirror(dst, base, from_lower=False):
    r = lax.broadcasted_iota(jnp.int32, (TILE, TILE), 0)
    c = lax.broadcasted_iota(jnp.int32, (TILE, TILE), 1)
    eye = jnp.where(r == c, 1.0, 0.0).astype(jnp.bfloat16)
    block_r, block_c = lax.shift_right_logical(r, 6), lax.shift_right_logical(c, 6)
    given = block_r > block_c if from_lower else block_r < block_c
    strict = jnp.where(given, 1.0, 0.0).astype(jnp.bfloat16)

    def tile_at(n, m):
        return (slice(base + n * TILE, base + (n + 1) * TILE), slice(m * TILE, (m + 1) * TILE))

    for n in range(WIDE // TILE):
        diag = dst[tile_at(n, n)]
        dst[tile_at(n, n)] = diag + dot(eye, diag * strict, NT).astype(jnp.bfloat16)
        for m in range(n + 1, WIDE // TILE):
            source, target = (tile_at(m, n), tile_at(n, m))
            if not from_lower:
                source, target = target, source
            dst[target] = dot(eye, dst[source], NT).astype(jnp.bfloat16)


def prepare_kernel(dens, mask, y, acc):
    q = lax.axis_index("depth")
    own_lower, own_upper = own_parts(dens, mask)

    @pl.when((q == 0) | (q == 2))
    def _():
        build(y, 0, None, own_upper)

    @pl.when(q == 2)
    def _():
        mirror(y, 0)

    @pl.when(q == 3)
    def _():
        build(y, 0, own_lower, None)

    @pl.when(q != 1)
    def _():
        for t in range(WIDE // TILE):
            lo, hi = t * TILE, (t + 1) * TILE
            acc[t, :, : WIDE - lo] = dot(y[lo:hi, :], y[lo:, :], NT)


def main_kernel(
    groups_half,
    dens,
    mask,
    y,
    acc,
    got_lower,
    got_depth,
    got_y,
    got_rest,
    own,
    first1,
    second1,
    first_free,
    second_free,
    first_due,
    second_due,
    z,
):
    q = lax.axis_index("depth")
    late = late_half(groups_half)
    own_lower, own_upper = own_parts(dens, mask)

    def finish(static_q, tile_row, window):
        for n in range(TILE // BS):
            i = tile_row * (TILE // BS) + n
            row = window[n * BS : (n + 1) * BS, n * BS : n * BS + WIDE].astype(jnp.bfloat16)

            def share(p):
                p = p % 4
                return row[:, p * TILE : (p + 1) * TILE]

            own[i] = share(static_q)
            first = jnp.where(late, share(static_q - 1), share(static_q + 1))
            second = jnp.where(late, share(static_q + 1), share(static_q - 1))
            if i < 8:
                first1[i] = share(static_q + 2)
                first_due[i] = first
                second_free[i] = second
            else:
                second1[i - 8] = share(static_q + 2)
                first_free[i - 8] = first
                second_due[i - 8] = second

    def products(static_q):
        for t in range(WIDE // TILE):
            lo, hi = t * TILE, (t + 1) * TILE
            ahead = acc[t, :, : WIDE - lo]
            if static_q == 3:
                later = dot(y[lo:hi, :hi], z[WIDE : WIDE + hi, :hi], NT)
                window = jnp.concatenate([ahead, later], axis=1)
            else:
                window = dot(z[lo:hi, :], z[lo : lo + WIDE + TILE, :], NT)
                later = window[:, WIDE - lo :]
                if static_q == 2:
                    later = later + dot(y[lo:hi, :], z[:WIDE, :hi], NN)
                window = jnp.concatenate([window[:, : WIDE - lo] + ahead, later], axis=1)
            finish(static_q, t, window)

    @pl.when(q == 0)
    def _():
        build(z, 0, own_lower, sent_upper(got_depth), packed_upper=True)
        build(z, WIDE, None, sent_upper(got_y, got_rest), packed_upper=True)
        products(0)

    @pl.when(q == 1)
    def _():
        for ref in (own, first_free, second_free, first_due, second_due):
            ref[...] = jnp.zeros_like(ref)

    @pl.when(q == 2)
    def _():
        build(z, 0, own_lower, sent_upper(got_depth), packed_upper=True)
        build(z, WIDE, sent_lower(got_lower), None, packed_lower=True)
        put_diagonal(z, WIDE, got_rest)
        mirror(z, WIDE, True)
        products(2)

    @pl.when(q == 3)
    def _():
        build(z, WIDE, sent_lower(got_lower), sent_upper(got_y, got_rest), True, True)
        products(3)


def add_kernel(first, second, got_first, got_second, first_out, second_out):
    for i in range(8):
        total = first[i].astype(jnp.float32) + got_first[i].astype(jnp.float32)
        first_out[i] = total.astype(jnp.bfloat16)
        total = second[i].astype(jnp.float32) + got_second[i].astype(jnp.float32)
        second_out[i] = total.astype(jnp.bfloat16)


def final_kernel(own, first_free, second_free, first_due, second_due, keep, out, mask):
    mask[...] = expand(keep[...], TILE)
    for i in range(ROWS):
        one, other = (first_due, second_free) if i < 8 else (first_free, second_due)
        total = own[i].astype(jnp.float32) + one[i % 8].astype(jnp.float32)
        total = total + other[i % 8].astype(jnp.float32)
        out[i] = (total * mask[i : i + 1, :]).astype(jnp.bfloat16)


def vmem(count):
    return [pl.BlockSpec(memory_space=pltpu.VMEM)] * count


def per_device(groups, density, pattern, keep_filter):
    mib = 1024 * 1024
    window_rows = (WIDE // TILE, TILE, WIDE)
    slot_mask = (ROWS, WIDE)
    wide_types = (window_rows, slot_mask)

    def call(kernel, outs, scratch, limit, flops, moved, *operands):
        return pl.pallas_call(
            kernel,
            out_shape=tuple(
                jax.ShapeDtypeStruct(shape, jnp.float32 if shape in wide_types else jnp.bfloat16)
                for shape in outs
            ),
            in_specs=vmem(len(operands)),
            out_specs=tuple(vmem(len(outs))),
            scratch_shapes=scratch,
            compiler_params=pltpu.CompilerParams(vmem_limit_bytes=limit * mib),
            cost_estimate=pl.CostEstimate(flops=flops, bytes_accessed=moved, transcendentals=0),
        )(*operands)

    upper_part = (17, BS, HALF)
    lower_part = (15, BS, HALF)
    share = (ROWS, BS, TILE)
    half_share = (ROWS // 2, BS, TILE)
    half = groups // 2

    upper, rest, mask = call(
        pack_kernel,
        ((MAIN, BS, HALF), (17 - MAIN, BS, HALF), slot_mask),
        [],
        16,
        4_000_000,
        3_500_000,
        density,
        pattern,
    )
    lower, upper_first = call(
        pack_first_kernel,
        (lower_part, upper_part),
        [],
        16,
        4_000_000,
        4_500_000,
        density,
        mask,
    )
    prepared, ahead = call(
        prepare_kernel,
        ((WIDE, WIDE), window_rows),
        [],
        16,
        3_000_000_000,
        9_500_000,
        density,
        mask,
    )

    def device(g, q):
        return (g % groups) * 4 + q

    of_lower, by_depth, by_y, of_rest, first_route, second_route = [], [], [], [], [], []
    for g in range(groups):
        of_lower += [(device(g, 1), device(g - 1, 2)), (device(g, 2), device(g - 1, 3))]
        by_depth += [(device(g, 1), device(g, 0)), (device(g, 3), device(g, 2))]
        by_y += [(device(g, 0), device(g - 1, 0)), (device(g, 3), device(g - 1, 3))]
        of_rest += by_y[-2:] + [(device(g, 2), device(g - 1, 2))]
        for q in range(4):
            up = (device(g, q), device(g, (q + 1) % 4))
            down = (device(g, q), device(g, (q - 1) % 4))
            first_route.append(down if g >= half else up)
            second_route.append(up if g >= half else down)
    got_lower = lax.ppermute(lower, AXES, of_lower)
    got_depth = lax.ppermute(upper_first, AXES, by_depth)
    got_y = lax.ppermute(upper, AXES, by_y)
    got_rest = lax.ppermute(rest, AXES, of_rest)

    own, first1, second1, first_free, second_free, first_due, second_due = call(
        functools.partial(main_kernel, half),
        (share,) + (half_share,) * 6,
        [pltpu.VMEM((2 * WIDE, WIDE), jnp.bfloat16)],
        20,
        6_000_000_000,
        14_000_000,
        density,
        mask,
        prepared,
        ahead,
        got_lower,
        got_depth,
        got_y,
        got_rest,
    )

    got_first = lax.ppermute(first1, AXES, [r for r in first_route if r[0] % 4 != 1])
    got_second = lax.ppermute(second1, AXES, [r for r in second_route if r[0] % 4 != 1])
    first_free = lax.ppermute(first_free, AXES, [r for r in first_route if r[0] % 4 != 1])
    second_free = lax.ppermute(second_free, AXES, [r for r in second_route if r[0] % 4 != 1])
    first_due, second_due = call(
        add_kernel,
        (half_share,) * 2,
        [],
        16,
        1_000_000,
        3_000_000,
        first_due,
        second_due,
        got_first,
        got_second,
    )
    first_due = lax.ppermute(first_due, AXES, first_route)
    second_due = lax.ppermute(second_due, AXES, second_route)
    (out,) = call(
        final_kernel,
        (share,),
        [pltpu.VMEM((ROWS, TILE), jnp.float32)],
        16,
        1_500_000,
        2_700_000,
        own,
        first_free,
        second_free,
        first_due,
        second_due,
        keep_filter,
    )
    return out


def solution(mesh):
    placed = (
        P(("row", "col"), None, "depth"),
        P(("row", "col"), "depth"),
        P(("row", "col"), "depth"),
    )
    groups = mesh.shape["row"] * mesh.shape["col"]
    return jax.shard_map(
        functools.partial(per_device, groups),
        mesh=mesh,
        in_specs=placed,
        out_specs=P(("row", "col"), None, "depth"),
        check_vma=False,
    )
```
